32 devices in a mesh: grp: 2 (over y), node: 4 (over z), sub: 2 (over x), rep: 2 (over core).
Axes of the slice: x: 2, y: 2, z: 4, core: 2. Of those that a mesh axis runs over, the one named last changes fastest.
Arguments:
- meson_nodes: float32 [2, 16, 512, 512], P(None, ('grp', 'node'), 'sub', 'rep'), parts along dimension 1, may hold values from -0.66 to 0.66
- term_nodes: int32 [8, 2], P('grp'), parts along dimension 0, may hold values from 0 to 7, as said below
- weight_codes: int32 [8], P('grp'), parts along dimension 0, may hold values from 0 to 7
- resident_pick: int32 [16], P('grp'), parts along dimension 0, may hold values from 0 to 1
Outputs:
- contracted: float32 [2, 16, 512, 512], P(None, ('grp', 'node'), 'sub', 'rep'), parts along dimension 1
The draws below stay inside these ranges and needn't reach their ends.
There are 2 independent parts, one for each index of `grp`. The reference program is written for one: setup_inputs(seed, part) draws one part's arguments, and reference() takes and returns one part's arrays. A program takes and returns all parts, laid end to end along the dimension named above; each array names one. Nothing has to cross between parts.
Inputs may be any that keep to these rules, and one draw needn't show every extreme that they name: `term_nodes`: node n belongs to owner n // 2. In every term the two nodes differ. The first nodes of at most 2 terms belong to any one owner, and those of exactly 2 terms to some owner.
All inputs are finite; a program needn't handle non-finite values.
Results may differ from the reference program's by a relative error of at most 0.000098.
Values sent between devices are 32-bit elements; how exact they have to be, the bound alone decides.
No kernel may reach another device: no remote copies, remote signals or barrier semaphores. Data moves between devices by JAX's collectives and lax.ppermute only.
A program may use at most 64 MiB of HBM per device.

```python
import jax
import jax.numpy as jnp
from jax import lax

NODE_DEV = 2
ORDER = 512
SLOTS = 2
NODES = 8
TERMS = 4


def draw_term_nodes(key, part):
    owners = NODES // NODE_DEV
    key_bias, key_jitter, key_hot, key_order, key_local, key_other = jax.random.split(key, 6)
    levels = jax.random.randint(key_bias, (owners, 1), 0, 4) * 1024
    jitter = jax.random.randint(key_jitter, (owners, SLOTS), 0, 1024)
    hottest = jax.random.randint(key_hot, (), 0, owners)
    owner_grid = jnp.arange(owners, dtype=jnp.int32)[:, None] * jnp.ones((1, SLOTS), jnp.int32)
    scores = jnp.where(owner_grid == hottest, 4096, levels + jitter)
    unique = scores * (owners * SLOTS) + jnp.arange(owners * SLOTS, dtype=jnp.int32).reshape(owners, SLOTS)
    chosen = lax.top_k(unique.reshape(-1), TERMS)[1]
    shuffled = jax.random.permutation(key_order, chosen)
    leading = shuffled // SLOTS * NODE_DEV + jax.random.randint(key_local, (TERMS,), 0, NODE_DEV)
    second = (leading + 1 + jax.random.randint(key_other, (TERMS,), 0, NODES - 1)) % NODES
    return jnp.stack([leading, second], axis=1).astype(jnp.int32)


def set_ends(result, own_key, least, largest):
    longest = result.shape.index(max(result.shape))
    spots = []
    for shift in (0, 1):
        where = [jax.random.randint(jax.random.fold_in(own_key, axis), (), 0, length) for axis, length in enumerate(result.shape)]
        where[longest] = (where[longest] + shift) % result.shape[longest]
        spots.append(tuple(where))
    return result.at[spots[0]].set(least).at[spots[1]].set(largest)


def shard_levels(rng, dims, cuts, low, largest):
    gain, own = 1.0, jax.random.fold_in(rng, 6)
    for axis_at, shards_of in cuts:
        heights = jnp.exp(jax.random.uniform(jax.random.fold_in(own, axis_at), (shards_of,), jnp.float32, low / len(cuts), largest / len(cuts)))
        gain = gain * jnp.repeat(heights, dims[axis_at] // shards_of).reshape([-1 if axis == axis_at else 1 for axis in range(len(dims))])
    return gain


def centred(stream_key, shape, deviation, limit, cuts=(), kind=jnp.bfloat16):
    gain = shard_levels(stream_key, shape, cuts, -0.22, 0.18) if cuts else 1.0
    drawn = jax.random.normal(stream_key, shape, jnp.float32) * deviation * gain
    return jnp.minimum(jnp.maximum(drawn, -limit), limit).astype(kind)


def setup_inputs(seed: int = 0, part: int = 0) -> dict:
    key_of = jax.random.split(jax.random.key(seed), 5)
    part_splits = jax.random.split(jax.random.fold_in(key_of[4], part), 5)
    return {
        "meson_nodes": centred(part_splits[0], (2, NODES, ORDER, ORDER), 0.096, 0.66, ((1, 4), (2, 2), (3, 2)), jnp.float32),
        "term_nodes": draw_term_nodes(jax.random.fold_in(jax.random.fold_in(key_of[4], part), 71), part),
        "weight_codes": set_ends(jax.random.randint(part_splits[2], (TERMS,), 0, 8), jax.random.fold_in(part_splits[2], 1), 0, 7).astype(jnp.int32),
        "resident_pick": set_ends(jax.random.randint(part_splits[3], (NODES,), 0, NODE_DEV), jax.random.fold_in(part_splits[3], 1), 0, NODE_DEV - 1).astype(jnp.int32),
    }


def complex_product(left_matrix, right_matrix):
    highest = lax.Precision.HIGHEST
    real_part = jnp.dot(left_matrix[0], right_matrix[0], precision=highest, preferred_element_type=jnp.float32) - jnp.dot(left_matrix[1], right_matrix[1], precision=highest, preferred_element_type=jnp.float32)
    imag_part = jnp.dot(left_matrix[0], right_matrix[1], precision=highest, preferred_element_type=jnp.float32) + jnp.dot(left_matrix[1], right_matrix[0], precision=highest, preferred_element_type=jnp.float32)
    return jnp.stack([real_part, imag_part])


def reference(meson_nodes, term_nodes, weight_codes, resident_pick):
    factors = (weight_codes.astype(jnp.float32) - 3.5) * 0.5

    def one_term(pair_ids):
        return complex_product(meson_nodes[:, pair_ids[0]], meson_nodes[:, pair_ids[1]])

    products = lax.map(one_term, term_nodes)
    node_ids = jnp.arange(NODES, dtype=jnp.int32)
    incidence = (term_nodes[:, 0:1] == node_ids[None, :]).astype(jnp.float32) + (term_nodes[:, 1:2] == node_ids[None, :]).astype(jnp.float32)
    mixing = factors[:, None] * incidence
    summed = jnp.einsum("tn,tcij->cnij", mixing, products, precision=lax.Precision.HIGHEST)
    resident = (node_ids // NODE_DEV) * NODE_DEV + resident_pick

    def one_node(node_index):
        return complex_product(summed[:, node_index], meson_nodes[:, resident[node_index]])

    contracted = lax.map(one_node, node_ids)
    return jnp.transpose(contracted, (1, 0, 2, 3))
```

```python
import functools

import jax
import jax.numpy as jnp
from jax import lax
from jax.experimental import pallas as pl
from jax.experimental.pallas import tpu as pltpu
from jax.sharding import PartitionSpec as P

VMEM_BYTES = 48 * 2**20
UNROLLED = 3
FIRST_OVER = 2


def round_bound(line, owned, terms):
    most = min(terms, owned)
    for hop in range(2, line):
        most = max(min(terms, owned * hop), most + 1)
    return max(most, FIRST_OVER) + terms


def plan_kernel(line, owned, terms, rounds, lead_ref, trail_ref, table_ref, length_ref):
    count = line * owned
    shape = (line, count)
    ids = lax.broadcasted_iota(jnp.int32, shape, 1)
    place = lax.broadcasted_iota(jnp.int32, shape, 0)
    home = ids // owned
    lowest, highest = home, home
    wanted = jnp.zeros(shape, jnp.float32)
    for t in range(terms):
        a, b = lead_ref[t], trail_ref[t]
        first_home, second_home = a // owned, b // owned
        other = jnp.where(ids == a, second_home, jnp.where(ids == b, first_home, home))
        lowest = jnp.minimum(lowest, other)
        highest = jnp.maximum(highest, other)
        wanted = jnp.where((place == first_home) & (ids == b) & (home != place), 1.0, wanted)

    def pick(score):
        best = jnp.max(score, axis=1, keepdims=True)
        chosen = jnp.where((score == best) & (score > 0.0), 1.0, 0.0)
        return best, chosen, jnp.sum(chosen * (ids - count).astype(jnp.float32), axis=1, keepdims=True) + float(count)

    def anywhere(chosen):
        return jnp.max(chosen, axis=0, keepdims=True).astype(jnp.int32)

    left, right = home, home
    lane = lax.broadcasted_iota(jnp.int32, (line, 2), 1)
    length = jnp.zeros((line, 2), jnp.int32)
    for step in range(rounds):
        to_go = jnp.where((left == place) & (lowest < place), place - lowest, 0)
        best_left, moved_left, send_left = pick(jnp.where(to_go > 0, (to_go + 1) * count - ids, 0).astype(jnp.float32))
        to_go = jnp.where((right == place) & (highest > place), highest - place, 0)
        best_right, moved_right, send_right = pick(jnp.where(to_go > 0, (to_go + 1) * count - ids, 0).astype(jnp.float32))
        busy_line = jnp.max(jnp.maximum(best_left, best_right), axis=0, keepdims=True)
        if step >= FIRST_OVER:
            here = ((left <= place) & (place < home)) | ((right >= place) & (place > home))
            best_over, moved_over, send_over = pick(jnp.where(here, wanted * (count - ids).astype(jnp.float32), 0.0))
            wanted = wanted - moved_over
            busy = jnp.maximum(busy_line, jnp.max(best_over, axis=0, keepdims=True))
        else:
            send_over, busy = jnp.full((line, 1), float(count), jnp.float32), busy_line
        for i, send in enumerate((send_left, send_right, send_over)):
            table_ref[3 * step + i] = send.astype(jnp.int32)
        left = left - anywhere(moved_left)
        right = right + anywhere(moved_right)
        length = jnp.where(jnp.where(lane == 0, busy_line, busy) > 0.0, step + 1, length)
    length_ref[...] = length


def plan_rounds(leading, trailing, line, owned, rounds):
    tables, lengths = pl.pallas_call(
        functools.partial(plan_kernel, line, owned, leading.shape[0], rounds),
        out_shape=[
            jax.ShapeDtypeStruct((3 * rounds, line, 1), jnp.int32),
            jax.ShapeDtypeStruct((line, 2), jnp.int32),
        ],
        in_specs=[pl.BlockSpec(memory_space=pltpu.SMEM)] * 2,
        out_specs=[pl.BlockSpec(memory_space=pltpu.VMEM)] * 2,
        cost_estimate=pl.CostEstimate(flops=1000, bytes_accessed=1000, transcendentals=0),
    )(leading, trailing)
    return tables.reshape(rounds, 3, line), lengths[0]


def split(value):
    high = value.astype(jnp.bfloat16)
    return high, (value - high.astype(jnp.float32)).astype(jnp.bfloat16)


def dot3(left, right):
    dot = functools.partial(jnp.dot, preferred_element_type=jnp.float32)
    return dot(left[0], right[0]) + (dot(left[0], right[1]) + dot(left[1], right[0]))


def product(left, right):
    return (
        dot3(left[0], right[0]) - dot3(left[1], right[1]),
        dot3(left[0], right[1]) + dot3(left[1], right[0]),
    )


def pair(high_ref, low_ref, n):
    return [(high_ref[n, c], low_ref[n, c]) for c in range(2)]


def put(high_ref, low_ref, n, c, rows, cols, value):
    high, low = split(value)
    high_ref[n, c, rows, cols] = high
    low_ref[n, c, rows, cols] = low


def block(index, size):
    return pl.ds(pl.multiple_of(index * size, size), size)


def mix_kernel(subs, items, weight_u_ref, weight_v_ref, weight_x_ref, *refs):
    own, across = refs[0], refs[1:subs]
    arrived, over = refs[subs : subs + items], refs[subs + items : 2 * subs + items - 1]
    u_ref, v_ref, x_refs = refs[2 * subs + items - 1], refs[2 * subs + items], refs[2 * subs + items + 1 :]
    owned = own.shape[1]
    for c in range(2):
        nodes = [own[c, m] for m in range(owned)] + [a[c] for a in arrived]
        for n in range(owned):
            u_ref[n, c] = sum(weight_u_ref[n, k] * node for k, node in enumerate(nodes))
            v_ref[n, c] = sum(weight_v_ref[n, k] * node for k, node in enumerate(nodes))
        for j in range(subs - 1):
            nodes = [across[j][c, m] for m in range(owned)] + [over[j][c]]
            for n in range(owned):
                x_refs[j][n, c] = sum(weight_x_ref[n, k] * node for k, node in enumerate(nodes))


def sum_kernel(subs, reps, where_ref, *refs):
    own, beside, across = refs[0], refs[1:reps], refs[reps : reps + subs - 1]
    u, v = refs[reps + subs - 1 : reps + 2 * subs - 1], refs[reps + 2 * subs - 1 : 2 * reps + 2 * subs - 1]
    out_ref, row_high, row_low, col_high, col_low, v_high, v_low, u_high, u_low = refs[2 * reps + 2 * subs - 1 :]
    rows, cols = out_ref.shape[2:]
    every = slice(None)
    for n in range(out_ref.shape[0]):
        for c in range(2):
            for i in range(reps):
                at = block(where_ref[subs + i], cols)
                put(row_high, row_low, n, c, every, at, (own if i == 0 else beside[i - 1])[c, n])
                put(v_high, v_low, n, c, every, at, v[i][n, c])
            for i in range(subs):
                at = block(where_ref[i], rows)
                put(col_high, col_low, n, c, at, every, (own if i == 0 else across[i - 1])[c, n])
                put(u_high, u_low, n, c, at, every, u[i][n, c])
        one = product(pair(row_high, row_low, n), pair(u_high, u_low, n))
        two = product(pair(v_high, v_low, n), pair(col_high, col_low, n))
        out_ref[n, 0] = one[0] + two[0]
        out_ref[n, 1] = one[1] + two[1]


def late_kernel(subs, where_ref, weight_ref, sum_ref, row_high, row_low, *refs):
    over, out_ref = refs[: subs - 1], refs[subs - 1]
    rows = sum_ref.shape[2]
    depth = row_high.shape[3] // subs
    for n in range(sum_ref.shape[0]):
        real, imag = sum_ref[n, 0], sum_ref[n, 1]
        for j in range(subs - 1):
            at = block(where_ref[1 + j], depth)
            left = [(row_high[n, c, :, at], row_low[n, c, :, at]) for c in range(2)]
            one = product(left, [split(weight_ref[n] * over[j][c]) for c in range(2)])
            real, imag = real + one[0], imag + one[1]
        out_ref[n, 0] = real
        out_ref[n, 1] = imag


def last_kernel(reps, cells, where_ref, pick_ref, col_high, col_low, *refs):
    s, (out_ref, s_high, s_low) = refs[:reps], refs[reps:]
    cols = out_ref.shape[3]
    for n in range(out_ref.shape[1]):
        for c in range(2):
            for i in range(reps):
                put(s_high, s_low, n, c, slice(None), block(where_ref[cells + i], cols), s[i][n, c])
        real, imag = product(pair(s_high, s_low, n), pair(col_high, col_low, pick_ref[n]))
        out_ref[0, n] = real
        out_ref[1, n] = imag


def call(kernel, scalars, arrays, outs, scratch=(), flops=0):
    moved = sum(a.size * a.dtype.itemsize for a in arrays)
    return pl.pallas_call(
        kernel,
        out_shape=outs,
        in_specs=[pl.BlockSpec(memory_space=pltpu.SMEM)] * len(scalars)
        + [pl.BlockSpec(memory_space=pltpu.VMEM)] * len(arrays),
        out_specs=jax.tree.map(lambda _: pl.BlockSpec(memory_space=pltpu.VMEM), outs),
        scratch_shapes=list(scratch),
        compiler_params=pltpu.CompilerParams(vmem_limit_bytes=VMEM_BYTES),
        cost_estimate=pl.CostEstimate(flops=flops, bytes_accessed=moved, transcendentals=0),
    )(*scalars, *arrays)


def shifts(array, axis):
    size = lax.axis_size(axis)
    return [lax.ppermute(array, axis, [(i, (i + j) % size) for i in range(size)]) for j in range(1, size)]


def places(axis):
    size = lax.axis_size(axis)
    return [(lax.axis_index(axis) - j) % size for j in range(size)]


def choose(index, nodes):
    value = nodes[0][1]
    for name, array in nodes[1:]:
        value = jnp.where(index == name, array, value)
    return value


def body(meson_nodes, term_nodes, weight_codes, resident_pick):
    line = lax.axis_size("node")
    subs, reps = lax.axis_size("sub"), lax.axis_size("rep")
    _, owned, rows, cols = meson_nodes.shape
    count = owned * line
    terms = term_nodes.shape[0]
    me = lax.axis_index("node")
    base = me * owned
    leading, trailing = term_nodes[:, 0], term_nodes[:, 1]
    to_left = [(z + 1, z) for z in range(line - 1)]
    to_right = [(z, z + 1) for z in range(line - 1)]

    tables, length = plan_rounds(leading, trailing, line, owned, round_bound(line, owned, terms))
    edges = jnp.pad(tables, ((0, 0), (0, 0), (1, 1)), constant_values=count)
    mine = lax.dynamic_slice_in_dim(edges, me, 3, axis=2)

    fixed = min(line - 1, UNROLLED)
    seen = [(base + m, meson_nodes[:, m]) for m in range(owned)]
    came = []
    over, across, beside = [], None, None
    for step in range(fixed):
        sent = [choose(mine[step, i, 1], seen) for i in range(2)]
        if step >= FIRST_OVER:
            sent.append(choose(mine[step, 2, 1], came))
        sent = lax.optimization_barrier(tuple(sent))
        from_right = lax.ppermute(sent[0], "node", to_left)
        from_left = lax.ppermute(sent[1], "node", to_right)
        if step >= FIRST_OVER:
            over.append(shifts(sent[2], "sub"))
        if step == 0:
            across, beside = shifts(meson_nodes, "sub"), shifts(meson_nodes, "rep")
            for other in shifts(length, "grp"):
                length = jnp.maximum(length, other)
        new = [(mine[step, 0, 2], from_right), (mine[step, 1, 0], from_left)]
        came = came + new
        seen = seen + new

    factors = (weight_codes.astype(jnp.float32) - 3.5) * 0.5
    mine_ids = base + jnp.arange(owned, dtype=jnp.int32)
    first_mine = factors[:, None] * (leading[:, None] == mine_ids)
    second_mine = factors[:, None] * (trailing[:, None] == mine_ids)

    def weights(mine_terms, others, names):
        return jnp.sum(mine_terms[:, :, None] * (others[:, None] == names)[:, None, :], axis=0)

    own_names = [base + m for m in range(owned)]
    names = jnp.stack(own_names + [name for name, _ in came])
    weight_u = weights(first_mine, trailing, names)
    weight_v = weights(second_mine, leading, names)
    weight_x = weights(first_mine, trailing, jnp.stack(own_names + [mine[step, 2, 1] for step in range(FIRST_OVER, fixed)]))
    where = jnp.stack([*places("sub"), *places("rep")]).astype(jnp.int32)
    picks = lax.dynamic_slice_in_dim(resident_pick, base, owned)
    nodes_shape = (owned, 2, rows, cols)
    depth = rows * subs
    flops = 3 * 8 * owned * rows * depth * cols

    def out(shape, dtype=jnp.float32):
        return jax.ShapeDtypeStruct(shape, dtype)

    def mixed():
        return call(
            functools.partial(mix_kernel, subs, len(came)),
            [weight_u, weight_v, weight_x],
            [meson_nodes, *across, *[array for _, array in came], *over[0]],
            [out(nodes_shape)] * (subs + 1),
        )

    def sums(u, v):
        row_part, col_part = (owned, 2, rows, depth), (owned, 2, depth, cols)
        scratch = [pltpu.VMEM(row_part, jnp.bfloat16)] * 2 + [pltpu.VMEM(col_part, jnp.bfloat16)] * 2
        return call(
            functools.partial(sum_kernel, subs, reps),
            [where],
            [meson_nodes, *beside, *across, *u, v, *shifts(v, "rep")],
            [out(nodes_shape)] + [out(row_part, jnp.bfloat16)] * 2 + [out(col_part, jnp.bfloat16)] * 2,
            scratch,
            2 * flops,
        )

    def finish(summed, col_high, col_low):
        scratch = [pltpu.VMEM((owned, 2, rows, depth), jnp.bfloat16)] * 2
        return call(
            functools.partial(last_kernel, reps, subs),
            [where, picks],
            [col_high, col_low, summed, *shifts(summed, "rep")],
            out(meson_nodes.shape),
            scratch,
            flops,
        )

    def short(_):
        index = mine[fixed, 2, 1]
        late = shifts(choose(index, came), "sub")
        u, v, *ux = mixed()
        summed, row_high, row_low, col_high, col_low = sums([u, *ux], v)
        weight_late = weights(first_mine, trailing, index[None])[:, 0]
        summed = call(
            functools.partial(late_kernel, subs),
            [where, weight_late],
            [summed, row_high, row_low, *late],
            out(nodes_shape),
            flops=flops // subs,
        )
        return finish(summed, col_high, col_low)

    def long(_):
        u, v, *ux = mixed()
        held = jnp.zeros((count + 1, 2, rows, cols), jnp.float32)
        for name, array in seen:
            held = lax.dynamic_update_slice_in_dim(held, array[None], name, 0)

        def add(total, mine_terms, others, name, item):
            return total + weights(mine_terms, others, name[None])[:, :, None, None] * item[None]

        def more(state):
            return state[0] < length[1]

        def again(state):
            step, held, u, v = state
            ids = lax.dynamic_index_in_dim(mine, step, 0, keepdims=False)
            left, right, item = lax.optimization_barrier(
                tuple(lax.dynamic_index_in_dim(held, ids[i, 1], 0, keepdims=False) for i in range(3))
            )
            from_right = lax.ppermute(left, "node", to_left)
            from_left = lax.ppermute(right, "node", to_right)
            items = [item, *shifts(item, "sub")]
            from_right, from_left = lax.optimization_barrier((from_right, from_left))
            u = [add(total, first_mine, trailing, ids[2, 1], x) for total, x in zip(u, items)]
            v = add(v, second_mine, leading, ids[0, 2], from_right)
            v = add(v, second_mine, leading, ids[1, 0], from_left)
            held = lax.dynamic_update_slice_in_dim(held, from_right[None], ids[0, 2], 0)
            held = lax.dynamic_update_slice_in_dim(held, from_left[None], ids[1, 0], 0)
            return step + 1, held, u, v

        gone = weights(first_mine, trailing, jnp.stack([mine[step, 2, 1] for step in range(FIRST_OVER, fixed)]))
        start = [
            sum(
                weight[:, k, None, None, None] * node[None]
                for weight, nodes in ((weight_u, [meson_nodes[:, m] for m in range(owned)]), (gone, [choose(mine[FIRST_OVER, 2, 1], came)]))
                for k, node in enumerate(nodes)
            ),
            *ux,
        ]
        _, _, u, v = lax.while_loop(more, again, (jnp.int32(fixed), held, start, v))
        summed, _, _, col_high, col_low = sums(u, v)
        return finish(summed, col_high, col_low)

    is_short = (length[0] <= fixed) & (length[1] <= fixed + 1)
    return lax.cond(is_short, short, long, None)


def solution(mesh):
    in_specs = (P(None, ("grp", "node"), "sub", "rep"), P("grp", None), P("grp"), P("grp"))
    out_specs = P(None, ("grp", "node"), "sub", "rep")
    return jax.shard_map(body, mesh=mesh, in_specs=in_specs, out_specs=out_specs, check_vma=False)
```

```python
import functools

import jax
import jax.numpy as jnp
from jax import lax
from jax.experimental import pallas as pl
from jax.experimental.pallas import tpu as pltpu
from jax.sharding import PartitionSpec as P

VMEM_BYTES = 24 * 2**20
UNROLLED = 3
FIRST_OVER = 2


def round_bound(line, owned, terms):
    most = min(terms, owned)
    for hop in range(2, line):
        most = max(min(terms, owned * hop), most + 1)
    return max(most, FIRST_OVER) + terms


def plan_kernel(line, owned, terms, rounds, opened, me_ref, terms_ref, codes_ref, slot_ref, weight_ref, table_ref, length_ref):
    count = line * owned
    shape = (line, count)
    ids = lax.broadcasted_iota(jnp.int32, shape, 1)
    place = lax.broadcasted_iota(jnp.int32, shape, 0)
    home = ids // owned
    lowest, highest = home, home
    wanted = jnp.zeros(shape, jnp.float32)
    me = me_ref[0]
    even = lax.rem(me, 2) == 0
    pairs = [(terms_ref[t, 0], terms_ref[t, 1]) for t in range(terms)]
    for a, b in pairs:
        first_home, second_home = a // owned, b // owned
        other = jnp.where(ids == a, second_home, jnp.where(ids == b, first_home, home))
        lowest = jnp.minimum(lowest, other)
        highest = jnp.maximum(highest, other)
        wanted = jnp.where((place == first_home) & (ids == b) & (home != place), 1.0, wanted)

    def pick(score):
        best = jnp.max(score, axis=1, keepdims=True)
        chosen = jnp.where((score == best) & (score > 0.0), 1.0, 0.0)
        return best, chosen, jnp.sum(chosen * (ids - count).astype(jnp.float32), axis=1, keepdims=True) + float(count)

    def anywhere(chosen):
        return jnp.max(chosen, axis=0, keepdims=True).astype(jnp.int32)

    rank = lax.broadcasted_iota(jnp.int32, (line, 1), 0)

    def of(send, who):
        return jnp.sum(jnp.where(rank == who, send - float(count), 0.0), axis=0, keepdims=True).astype(jnp.int32) + count

    names = [jnp.full((1, 1), me * owned + m, jnp.int32) for m in range(owned)]

    def write(row, send):
        wanted_name = of(send, me)
        slot = jnp.zeros((1, 1), jnp.int32)
        for k, name in enumerate(names):
            slot = jnp.where(wanted_name == name, k, slot)
        slot_ref[row] = jnp.broadcast_to(slot, slot_ref.shape[1:])
        return wanted_name

    left, right = home, home
    lane = lax.broadcasted_iota(jnp.int32, (line, 2), 1)
    length = jnp.zeros((line, 2), jnp.int32)
    gone = []
    for step in range(rounds):
        to_go = jnp.where((left == place) & (lowest < place), place - lowest, 0)
        best_left, moved_left, send_left = pick(jnp.where(to_go > 0, (to_go + 1) * count - ids, 0).astype(jnp.float32))
        to_go = jnp.where((right == place) & (highest > place), highest - place, 0)
        best_right, moved_right, send_right = pick(jnp.where(to_go > 0, (to_go + 1) * count - ids, 0).astype(jnp.float32))
        busy_line = jnp.max(jnp.maximum(best_left, best_right), axis=0, keepdims=True)
        if step >= FIRST_OVER:
            here = ((left <= place) & (place < home)) | ((right >= place) & (place > home))
            best_over, moved_over, send_over = pick(jnp.where(here, wanted * (count - ids).astype(jnp.float32), 0.0))
            wanted = wanted - moved_over
            busy = jnp.maximum(busy_line, jnp.max(best_over, axis=0, keepdims=True))
        else:
            send_over, busy = jnp.full((line, 1), float(count), jnp.float32), busy_line
        for i, send in enumerate((send_left, send_right, send_over)):
            table_ref[3 * step + i] = send.astype(jnp.int32)
        if step <= opened:
            first = jnp.where(even, send_right, send_left)
            second = jnp.where(even, send_left, send_right)
            for i, send in enumerate((first, second, send_over)):
                name = write(3 * step + i, send)
                if i == 2 and step >= FIRST_OVER:
                    gone.append(name)
            come_left, come_right = of(send_left, me + 1), of(send_right, me - 1)
            names += [jnp.where(even, come_left, come_right), jnp.where(even, come_right, come_left)]
        left = left - anywhere(moved_left)
        right = right + anywhere(moved_right)
        length = jnp.where(jnp.where(lane == 0, busy_line, busy) > 0.0, step + 1, length)
    length_ref[...] = length

    names = names[: owned + 2 * opened]
    row = 0
    for side, queue in ((0, names), (1, names), (0, gone)):
        for n in range(owned):
            scales = [
                jnp.where(ours[side] == me * owned + n, (codes_ref[t].astype(jnp.float32) - 3.5) * 0.5, 0.0)
                for t, ours in enumerate(pairs)
            ]
            for name in queue:
                weight = jnp.zeros((1, 1), jnp.float32)
                for scale, ours in zip(scales, pairs):
                    weight = weight + jnp.where(name == ours[1 - side], scale, 0.0)
                weight_ref[row] = jnp.broadcast_to(weight, weight_ref.shape[1:])
                row += 1


def plan_rounds(me, term_nodes, weight_codes, line, owned, rounds, opened, cols):
    overs = opened + 1 - FIRST_OVER
    rows = owned * (2 * (owned + 2 * opened) + overs)
    slots, weights, tables, lengths = pl.pallas_call(
        functools.partial(plan_kernel, line, owned, term_nodes.shape[0], rounds, opened),
        out_shape=[
            jax.ShapeDtypeStruct((3 * (opened + 1), 1, cols), jnp.int32),
            jax.ShapeDtypeStruct((rows, 1, cols), jnp.float32),
            jax.ShapeDtypeStruct((3 * rounds, line, 1), jnp.int32),
            jax.ShapeDtypeStruct((line, 2), jnp.int32),
        ],
        in_specs=[pl.BlockSpec(memory_space=pltpu.SMEM)] * 3,
        out_specs=[pl.BlockSpec(memory_space=pltpu.VMEM)] * 4,
        cost_estimate=pl.CostEstimate(flops=1000, bytes_accessed=1000, transcendentals=0),
    )(me, term_nodes, weight_codes)
    return slots, weights, tables.reshape(rounds, 3, line), lengths[0]


def split(value):
    high = value.astype(jnp.bfloat16)
    return high, (value - high.astype(jnp.float32)).astype(jnp.bfloat16)


def dot3(left, right):
    dot = functools.partial(jnp.dot, preferred_element_type=jnp.float32)
    return dot(left[0], right[0]) + (dot(left[0], right[1]) + dot(left[1], right[0]))


def product(left, right):
    return (
        dot3(left[0], right[0]) - dot3(left[1], right[1]),
        dot3(left[0], right[1]) + dot3(left[1], right[0]),
    )


def pair(high_ref, low_ref, n):
    return [(high_ref[n, c], low_ref[n, c]) for c in range(2)]


def put(high_ref, low_ref, n, c, rows, cols, value):
    high, low = split(value)
    high_ref[n, c, rows, cols] = high
    low_ref[n, c, rows, cols] = low


def block(index, size):
    return pl.ds(pl.multiple_of(index * size, size), size)


def choose_kernel(rows, owned, copies, slot_ref, *refs):
    outs = refs[len(refs) - len(rows) - copies :]
    own, arrived = refs[0], refs[1 : len(refs) - len(rows) - copies]
    for row, out_ref in zip(rows, outs):
        slot = jnp.broadcast_to(slot_ref[row], out_ref.shape[1:])
        for c in range(2):
            value = own[c, 0]
            for m in range(1, owned):
                value = jnp.where(slot == m, own[c, m], value)
            for k, node in enumerate(arrived):
                value = jnp.where(slot == owned + k, node[c], value)
            out_ref[c] = value
    for m in range(copies):
        for c in range(2):
            outs[len(rows) + m][c] = own[c, m]


def early_kernel(subs, reps, names, where_ref, weight_ref, *refs):
    outs = 2 + subs - 1 + 4
    refs, (u_ref, v_ref, *rest) = refs[: len(refs) - outs], refs[len(refs) - outs :]
    x_refs, (row_high, row_low, col_high, col_low) = rest[: subs - 1], rest[subs - 1 :]
    own, beside, refs = refs[0], refs[1:reps], refs[reps:]
    rows, cols = own.shape[2:]
    owned = own.shape[1]
    across = [refs[m * (subs - 1) : (m + 1) * (subs - 1)] for m in range(owned)]
    arrived = refs[owned * (subs - 1) :]
    every = slice(None)
    for n in range(owned):
        for c in range(2):
            for i in range(reps):
                at = block(where_ref[subs + i], cols)
                put(row_high, row_low, n, c, every, at, (own if i == 0 else beside[i - 1])[c, n])
            for i in range(subs):
                matrix = own[c, n] if i == 0 else across[n][i - 1][c]
                put(col_high, col_low, n, c, block(where_ref[i], rows), every, matrix)
            nodes = [own[c, m] for m in range(owned)] + [a[c] for a in arrived]
            u_ref[n, c] = sum(weight_ref[n * names + k] * node for k, node in enumerate(nodes))
            v_ref[n, c] = sum(weight_ref[(owned + n) * names + k] * node for k, node in enumerate(nodes))
            for j in range(subs - 1):
                x_refs[j][n, c] = sum(weight_ref[n * names + m] * across[m][j][c] for m in range(owned))


def mix_kernel(subs, names, seen, arrived, gone, weight_ref, u_ref, v_ref, *refs):
    x_refs, items, refs = refs[: subs - 1], refs[subs - 1 : subs - 1 + arrived], refs[subs - 1 + arrived :]
    over, (u_out, v_out, *x_outs) = refs[: len(refs) - subs - 1], refs[len(refs) - subs - 1 :]
    owned = u_ref.shape[0]
    for n in range(owned):
        for c in range(2):
            u, v = u_ref[n, c], v_ref[n, c]
            for k, item in enumerate(items):
                u = u + weight_ref[n * names + seen + k] * item[c]
                v = v + weight_ref[(owned + n) * names + seen + k] * item[c]
            u_out[n, c], v_out[n, c] = u, v
            for j in range(subs - 1):
                x = x_refs[j][n, c]
                for k in range(len(over) // (subs - 1)):
                    x = x + weight_ref[2 * owned * names + n * gone + k] * over[k * (subs - 1) + j][c]
                x_outs[j][n, c] = x


def sum_kernel(subs, reps, where_ref, row_high, row_low, col_high, col_low, *refs):
    u, v, (out_ref, v_high, v_low, u_high, u_low) = refs[:subs], refs[subs : subs + reps], refs[subs + reps :]
    rows, cols = out_ref.shape[2:]
    for n in range(out_ref.shape[0]):
        for c in range(2):
            for i in range(subs):
                put(u_high, u_low, n, c, block(where_ref[i], rows), slice(None), u[i][n, c])
            for i in range(reps):
                put(v_high, v_low, n, c, slice(None), block(where_ref[subs + i], cols), v[i][n, c])
        one = product(pair(row_high, row_low, n), pair(u_high, u_low, n))
        two = product(pair(v_high, v_low, n), pair(col_high, col_low, n))
        out_ref[n, 0] = one[0] + two[0]
        out_ref[n, 1] = one[1] + two[1]


def late_kernel(subs, first, stride, where_ref, weight_ref, sum_ref, row_high, row_low, *refs):
    over, out_ref = refs[: subs - 1], refs[subs - 1]
    rows = sum_ref.shape[2]
    depth = row_high.shape[3] // subs
    for n in range(sum_ref.shape[0]):
        real, imag = sum_ref[n, 0], sum_ref[n, 1]
        for j in range(subs - 1):
            at = block(where_ref[1 + j], depth)
            left = [(row_high[n, c, :, at], row_low[n, c, :, at]) for c in range(2)]
            one = product(left, [split(weight_ref[first + stride * n] * over[j][c]) for c in range(2)])
            real, imag = real + one[0], imag + one[1]
        out_ref[n, 0] = real
        out_ref[n, 1] = imag


def last_kernel(reps, cells, where_ref, pick_ref, col_high, col_low, *refs):
    s, (out_ref, s_high, s_low) = refs[:reps], refs[reps:]
    cols = out_ref.shape[3]
    for n in range(out_ref.shape[1]):
        for c in range(2):
            for i in range(reps):
                put(s_high, s_low, n, c, slice(None), block(where_ref[cells + i], cols), s[i][n, c])
        real, imag = product(pair(s_high, s_low, n), pair(col_high, col_low, pick_ref[n]))
        out_ref[0, n] = real
        out_ref[1, n] = imag


def call(kernel, scalars, arrays, outs, scratch=()):
    return pl.pallas_call(
        kernel,
        out_shape=outs,
        in_specs=[pl.BlockSpec(memory_space=pltpu.SMEM)] * len(scalars)
        + [pl.BlockSpec(memory_space=pltpu.VMEM)] * len(arrays),
        out_specs=jax.tree.map(lambda _: pl.BlockSpec(memory_space=pltpu.VMEM), outs),
        scratch_shapes=list(scratch),
        compiler_params=pltpu.CompilerParams(vmem_limit_bytes=VMEM_BYTES),
        cost_estimate=pl.CostEstimate(flops=1000, bytes_accessed=1000, transcendentals=0),
    )(*scalars, *arrays)


def shifts(array, axis):
    size = lax.axis_size(axis)
    return [lax.ppermute(array, axis, [(i, (i + j) % size) for i in range(size)]) for j in range(1, size)]


def places(axis):
    size = lax.axis_size(axis)
    return [(lax.axis_index(axis) - j) % size for j in range(size)]


def body(meson_nodes, term_nodes, weight_codes, resident_pick):
    line = lax.axis_size("node")
    subs, reps = lax.axis_size("sub"), lax.axis_size("rep")
    _, owned, rows, cols = meson_nodes.shape
    count = owned * line
    terms = term_nodes.shape[0]
    me = lax.axis_index("node")
    base = me * owned
    to_left = [(z + 1, z) for z in range(line - 1)]
    to_right = [(z, z + 1) for z in range(line - 1)]
    node_shape = (2, rows, cols)
    nodes_shape = (owned, 2, rows, cols)
    depth = rows * subs
    fixed = min(line - 1, UNROLLED)
    opened = fixed + 1

    def out(shape, dtype=jnp.float32):
        return jax.ShapeDtypeStruct(shape, dtype)

    slots, weights, tables, length = plan_rounds(
        me.reshape(1), term_nodes, weight_codes, line, owned, round_bound(line, owned, terms), opened, cols
    )

    names = owned + 2 * opened
    gone = opened + 1 - FIRST_OVER
    pairs = [[(z, z + 1) for z in range(start, line - 1, 2)] for start in range(2)]
    swaps = [pair + [(j, i) for i, j in pair] for pair in pairs]

    def choose(step, kinds, came, copies=0):
        return call(
            functools.partial(choose_kernel, [3 * step + kind for kind in kinds], owned, copies),
            [],
            [slots, meson_nodes, *came],
            [out(node_shape)] * (len(kinds) + copies),
        )

    def meet(first, second):
        return [lax.ppermute(item, "node", swap) for item, swap in zip((first, second), swaps)]

    own = None
    came, across, over = [], [], []
    for step in range(fixed):
        if step == 0:
            first, second, *own = choose(step, (0, 1), came, owned)
        elif step < FIRST_OVER:
            first, second = choose(step, (0, 1), came)
        else:
            first, second, *own = choose(step, (0, 1, 2), came)
        last = owned if step == FIRST_OVER - 1 else step + 1
        beyond = [x for item in (own[step:last] if step < FIRST_OVER else own) for x in shifts(item, "sub")]
        new, beyond = lax.optimization_barrier((meet(first, second), beyond))
        came = came + new
        if step < FIRST_OVER:
            across = across + beyond
        else:
            over = over + beyond
        if step == FIRST_OVER - 1:
            beside = shifts(meson_nodes, "rep")
            for other in shifts(length, "grp"):
                length = jnp.maximum(length, other)
            came, beside, length = lax.optimization_barrier((came, beside, length))
            before = len(came)

    where = jnp.stack([*places("sub"), *places("rep")]).astype(jnp.int32)
    picks = lax.dynamic_slice_in_dim(resident_pick, base, owned)

    row_part, col_part = (owned, 2, rows, depth), (owned, 2, depth, cols)
    *early, row_high, row_low, col_high, col_low = call(
        functools.partial(early_kernel, subs, reps, names),
        [where],
        [weights, meson_nodes, *beside, *across, *came[:before]],
        [out(nodes_shape)] * (subs + 1) + [out(row_part, jnp.bfloat16)] * 2 + [out(col_part, jnp.bfloat16)] * 2,
    )

    def mixed(came, over):
        return call(
            functools.partial(mix_kernel, subs, names, owned + before, len(came) - before, gone),
            [],
            [weights, *early, *came[before:], *over],
            [out(nodes_shape)] * (subs + 1),
        )

    def sums(u, v):
        scratch = [pltpu.VMEM(row_part, jnp.bfloat16)] * 2 + [pltpu.VMEM(col_part, jnp.bfloat16)] * 2
        return call(
            functools.partial(sum_kernel, subs, reps),
            [where],
            [row_high, row_low, col_high, col_low, *u, v, *shifts(v, "rep")],
            out(nodes_shape),
            scratch,
        )

    def finish(summed):
        scratch = [pltpu.VMEM(row_part, jnp.bfloat16)] * 2
        return call(
            functools.partial(last_kernel, reps, subs),
            [where, picks],
            [col_high, col_low, summed, *shifts(summed, "rep")],
            out(meson_nodes.shape),
            scratch,
        )

    def end(step, came, over):
        [item] = choose(step, (2,), came)
        late = shifts(item, "sub")
        item, came, over = lax.optimization_barrier((item, came, over))
        u, v, *ux = mixed(came, over)
        first = 2 * owned * names + step - FIRST_OVER
        summed = call(
            functools.partial(late_kernel, subs, first, gone),
            [where],
            [weights, sums([u, *ux], v), row_high, row_low, *late],
            out(nodes_shape),
        )
        return finish(summed)

    def short(_):
        return end(fixed, came, over)

    def middle(_):
        first, second, item = choose(fixed, (0, 1, 2), came)
        new, beyond = lax.optimization_barrier((meet(first, second), shifts(item, "sub")))
        return end(fixed + 1, came + new, over + beyond)

    def long(_):
        edges = jnp.pad(tables, ((0, 0), (0, 0), (1, 1)), constant_values=count)
        mine = lax.dynamic_slice_in_dim(edges, me, 3, axis=2)
        leading, trailing = term_nodes[:, 0], term_nodes[:, 1]
        factors = (weight_codes.astype(jnp.float32) - 3.5) * 0.5
        mine_ids = base + jnp.arange(owned, dtype=jnp.int32)
        first_mine = factors[:, None] * (leading[:, None] == mine_ids)
        second_mine = factors[:, None] * (trailing[:, None] == mine_ids)
        is_even = me % 2 == 0
        from_right, from_left = [mine[step, 0, 2] for step in range(fixed)], [mine[step, 1, 0] for step in range(fixed)]
        arrivals = []
        for right, left in zip(from_right, from_left):
            arrivals += [jnp.where(is_even, right, left), jnp.where(is_even, left, right)]
        held = jnp.zeros((count + 1, 2, rows, cols), jnp.float32)
        held = lax.dynamic_update_slice(held, jnp.swapaxes(meson_nodes, 0, 1), (base, 0, 0, 0))
        for name, array in zip(arrivals, came):
            held = lax.dynamic_update_slice_in_dim(held, array[None], name, 0)

        def add(total, mine_terms, others, name, item):
            scale = jnp.sum(mine_terms * (others == name)[:, None], axis=0)
            return total + scale[:, None, None, None] * item[None]

        def take(name):
            return lax.dynamic_index_in_dim(held, name, 0, keepdims=False)

        u = [jnp.zeros(nodes_shape, jnp.float32)] * subs
        v = jnp.zeros(nodes_shape, jnp.float32)
        for m in range(owned):
            beyond = across[m * (subs - 1) : (m + 1) * (subs - 1)]
            u = [add(total, first_mine, trailing, base + m, x) for total, x in zip(u, (meson_nodes[:, m], *beyond))]
            v = add(v, second_mine, leading, base + m, meson_nodes[:, m])
        for name, array in zip(arrivals, came):
            v = add(v, second_mine, leading, name, array)
        for step in range(FIRST_OVER, fixed):
            name = mine[step, 2, 1]
            there = over[(step - FIRST_OVER) * (subs - 1) :][: subs - 1]
            u = [add(total, first_mine, trailing, name, x) for total, x in zip(u, (take(name), *there))]

        def more(state):
            return state[0] < length[1]

        def again(state):
            step, held, u, v = state
            ids = lax.dynamic_index_in_dim(mine, step, 0, keepdims=False)
            left, right, item = lax.optimization_barrier(
                tuple(lax.dynamic_index_in_dim(held, ids[i, 1], 0, keepdims=False) for i in range(3))
            )
            from_right = lax.ppermute(left, "node", to_left)
            from_left = lax.ppermute(right, "node", to_right)
            items = [item, *shifts(item, "sub")]
            from_right, from_left = lax.optimization_barrier((from_right, from_left))
            u = [add(total, first_mine, trailing, ids[2, 1], x) for total, x in zip(u, items)]
            v = add(v, second_mine, leading, ids[0, 2], from_right)
            v = add(v, second_mine, leading, ids[1, 0], from_left)
            held = lax.dynamic_update_slice_in_dim(held, from_right[None], ids[0, 2], 0)
            held = lax.dynamic_update_slice_in_dim(held, from_left[None], ids[1, 0], 0)
            return step + 1, held, u, v

        _, _, u, v = lax.while_loop(more, again, (jnp.int32(fixed), held, u, v))
        return finish(sums(u, v))

    way = jnp.maximum(length[0] - fixed, length[1] - fixed - 1)
    return lax.switch(jnp.clip(way, 0, 2), [short, middle, long], None)


def solution(mesh):
    in_specs = (P(None, ("grp", "node"), "sub", "rep"), P("grp", None), P("grp"), P("grp"))
    out_specs = P(None, ("grp", "node"), "sub", "rep")
    return jax.shard_map(body, mesh=mesh, in_specs=in_specs, out_specs=out_specs, check_vma=False)
```

```python
import functools

import jax
import jax.numpy as jnp
from jax import lax
from jax.experimental import pallas as pl
from jax.experimental.pallas import tpu as pltpu
from jax.sharding import PartitionSpec as P

VMEM_BYTES = 20 * 2**20
UNROLLED = 3
FIRST_OVER = 2


def round_bound(line, owned, terms):
    most = min(terms, owned)
    for hop in range(2, line):
        most = max(min(terms, owned * hop), most + 1)
    return max(most, FIRST_OVER) + terms


def plan_kernel(line, owned, terms, rounds, opened, *refs):
    place_ref, all_terms_ref, codes_ref, slot_ref, weight_ref, table_ref, length_ref, terms_ref, sem = refs
    fetch(all_terms_ref, terms_ref, sem)
    count = line * owned
    shape = (line, count)
    ids = lax.broadcasted_iota(jnp.int32, shape, 1)
    place = lax.broadcasted_iota(jnp.int32, shape, 0)
    home = ids // owned
    lowest, highest = home, home
    wanted = jnp.zeros(shape, jnp.float32)
    me = place_ref[0]
    even = lax.rem(me, 2) == 0
    pairs = [(terms_ref[0, t], terms_ref[1, t]) for t in range(terms)]
    for a, b in pairs:
        first_home, second_home = a // owned, b // owned
        other = jnp.where(ids == a, second_home, jnp.where(ids == b, first_home, home))
        lowest = jnp.minimum(lowest, other)
        highest = jnp.maximum(highest, other)
        wanted = jnp.where((place == first_home) & (ids == b) & (home != place), 1.0, wanted)

    def pick(score):
        best = jnp.max(score, axis=1, keepdims=True)
        chosen = jnp.where((score == best) & (score > 0.0), 1.0, 0.0)
        return best, chosen, jnp.sum(chosen * (ids - count).astype(jnp.float32), axis=1, keepdims=True) + float(count)

    def anywhere(chosen):
        return jnp.max(chosen, axis=0, keepdims=True).astype(jnp.int32)

    rank = lax.broadcasted_iota(jnp.int32, (line, 1), 0)

    def of(send, who):
        return jnp.sum(jnp.where(rank == who, send - float(count), 0.0), axis=0, keepdims=True).astype(jnp.int32) + count

    names = [jnp.full((1, 1), me * owned + m, jnp.int32) for m in range(owned)]

    def write(row, send):
        wanted_name = of(send, me)
        slot = jnp.zeros((1, 1), jnp.float32)
        for k, name in enumerate(names):
            slot = jnp.where(wanted_name == name, float(k), slot)
        slot_ref[row] = jnp.broadcast_to(slot, slot_ref.shape[1:])
        return wanted_name

    left, right = home, home
    lane = lax.broadcasted_iota(jnp.int32, (line, 2), 1)
    length = jnp.zeros((line, 2), jnp.int32)
    gone = []
    for step in range(rounds):
        to_go = jnp.where((left == place) & (lowest < place), place - lowest, 0)
        best_left, moved_left, send_left = pick(jnp.where(to_go > 0, (to_go + 1) * count - ids, 0).astype(jnp.float32))
        to_go = jnp.where((right == place) & (highest > place), highest - place, 0)
        best_right, moved_right, send_right = pick(jnp.where(to_go > 0, (to_go + 1) * count - ids, 0).astype(jnp.float32))
        busy_line = jnp.max(jnp.maximum(best_left, best_right), axis=0, keepdims=True)
        if step >= FIRST_OVER:
            here = ((left <= place) & (place < home)) | ((right >= place) & (place > home))
            best_over, moved_over, send_over = pick(jnp.where(here, wanted * (count - ids).astype(jnp.float32), 0.0))
            wanted = wanted - moved_over
            busy = jnp.maximum(busy_line, jnp.max(best_over, axis=0, keepdims=True))
        else:
            send_over, busy = jnp.full((line, 1), float(count), jnp.float32), busy_line
        for i, send in enumerate((send_left, send_right, send_over)):
            table_ref[3 * step + i] = send.astype(jnp.int32)
        if step <= opened:
            first = jnp.where(even, send_right, send_left)
            second = jnp.where(even, send_left, send_right)
            for i, send in enumerate((first, second, send_over)):
                name = write(3 * step + i, send)
                if i == 2 and step >= FIRST_OVER:
                    gone.append(name)
            come_left, come_right = of(send_left, me + 1), of(send_right, me - 1)
            names += [jnp.where(even, come_left, come_right), jnp.where(even, come_right, come_left)]
        left = left - anywhere(moved_left)
        right = right + anywhere(moved_right)
        length = jnp.where(jnp.where(lane == 0, busy_line, busy) > 0.0, step + 1, length)
    length_ref[0] = jnp.max(length[:, :1].astype(jnp.float32)).astype(jnp.int32)
    length_ref[1] = jnp.max(length[:, 1:].astype(jnp.float32)).astype(jnp.int32)

    names = names[: owned + 2 * opened]
    row = 0
    for side, queue in ((0, names), (1, names), (0, gone)):
        for n in range(owned):
            scales = [
                jnp.where(ours[side] == me * owned + n, (codes_ref[t].astype(jnp.float32) - 3.5) * 0.5, 0.0)
                for t, ours in enumerate(pairs)
            ]
            for name in queue:
                weight = jnp.zeros((1, 1), jnp.float32)
                for scale, ours in zip(scales, pairs):
                    weight = weight + jnp.where(name == ours[1 - side], scale, 0.0)
                weight_ref[row] = jnp.broadcast_to(weight, weight_ref.shape[1:])
                row += 1


def plan_rounds(me, term_nodes, weight_codes, line, owned, rounds, opened, cols):
    overs = opened + 1 - FIRST_OVER
    rows = owned * (2 * (owned + 2 * opened) + overs)
    slots, weights, tables, lengths = pl.pallas_call(
        functools.partial(plan_kernel, line, owned, term_nodes.shape[1], rounds, opened),
        out_shape=[
            jax.ShapeDtypeStruct((3 * (opened + 1), 1, 128), jnp.float32),
            jax.ShapeDtypeStruct((rows, 1, cols), jnp.float32),
            jax.ShapeDtypeStruct((3 * rounds, line, 1), jnp.int32),
            jax.ShapeDtypeStruct((2,), jnp.int32),
        ],
        in_specs=[pl.BlockSpec(memory_space=space) for space in (pltpu.SMEM, pl.ANY, pltpu.SMEM)],
        scratch_shapes=[pltpu.SMEM(term_nodes.shape, jnp.int32), pltpu.SemaphoreType.DMA],
        out_specs=[pl.BlockSpec(memory_space=pltpu.VMEM)] * 3 + [pl.BlockSpec(memory_space=pltpu.SMEM)],
        cost_estimate=pl.CostEstimate(flops=1000, bytes_accessed=1000, transcendentals=0),
    )(me, term_nodes, weight_codes)
    return slots, weights, tables, lengths


def split(value):
    high = value.astype(jnp.bfloat16)
    return high, (value - high.astype(jnp.float32)).astype(jnp.bfloat16)


def product(left, right_real, right_imag):
    rows = left.shape[2]
    every = left.reshape(4 * rows, left.shape[3])
    dot = functools.partial(jnp.dot, preferred_element_type=jnp.float32)

    def times(high, low):
        one, two = dot(every, high), dot(every[: 2 * rows], low)
        both = one[: 2 * rows] + (one[2 * rows :] + two)
        return both[:rows], both[rows:]

    real_real, imag_real = times(*right_real)
    real_imag, imag_imag = times(*right_imag)
    return real_real - imag_imag, real_imag + imag_real


def put_left(ref, n, c, cols, value):
    for part, piece in enumerate(split(value)):
        ref[n, part, c, :, cols] = piece


def put_right(ref, n, c, rows, value):
    for part, piece in enumerate(split(value)):
        ref[n, c, part, rows, :] = piece


def right_parts(ref, n):
    return [(ref[n, c, 0], ref[n, c, 1]) for c in range(2)]


def block(index, size):
    return pl.ds(pl.multiple_of(index * size, size), size)


def fetch(terms_ref, terms_here, sem):
    copy = pltpu.make_async_copy(terms_ref, terms_here, sem)
    copy.start()
    copy.wait()


def copy_chosen(slots, nodes, outs, sems):
    for i, (slot, out_ref) in enumerate(zip(slots, outs)):
        for k, node in enumerate(nodes):

            @pl.when(slot == k)
            def _(node=node, out_ref=out_ref, i=i):
                pltpu.make_async_copy(node, out_ref, sems.at[i]).start()

    return [pltpu.make_async_copy(nodes[0], out_ref, sems.at[i]) for i, out_ref in enumerate(outs)]


def first_kernel(line, owned, terms, place_ref, terms_ref, own_ref, first_ref, second_ref, *refs):
    copies, (terms_here, sem, sems) = refs[:owned], refs[owned:]
    moves = [
        pltpu.make_async_copy(own_ref.at[c, m], copies[m].at[c], sems.at[c, m]) for m in range(owned) for c in range(2)
    ]
    fetch = pltpu.make_async_copy(terms_ref, terms_here, sem)
    for move in [fetch, *moves]:
        move.start()
    fetch.wait()
    me = place_ref[0]
    choice = []
    lows, highs = [jnp.int32(0)] * owned, [jnp.int32(0)] * owned
    for t in range(terms):
        a, b = terms_here[0, t], terms_here[1, t]
        to_second, to_first = b // owned - me, a // owned - me
        for m in range(owned):
            name = me * owned + m
            away = jnp.where(a == name, to_second, jnp.where(b == name, to_first, 0))
            lows[m] = jnp.maximum(lows[m], -away)
            highs[m] = jnp.maximum(highs[m], away)
    for far in (lows, highs):
        best, slot = far[0], jnp.int32(0)
        for m in range(1, owned):
            slot = jnp.where(far[m] > best, m, slot)
            best = jnp.maximum(far[m], best)
        choice.append(slot)
    even = lax.rem(me, 2) == 0
    slots = (jnp.where(even, choice[1], choice[0]), jnp.where(even, choice[0], choice[1]))
    for move in moves:
        move.wait()
    for slot, out_ref in zip(slots, (first_ref, second_ref)):
        for m in range(owned):

            @pl.when(slot == m)
            def _(m=m, out_ref=out_ref):
                out_ref[...] = copies[m][...]


def choose_kernel(rows, slot_ref, *refs):
    count = len(refs) - 1 - len(rows)
    slots = [jnp.max(slot_ref[row]).astype(jnp.int32) for row in rows]
    for copy in copy_chosen(slots, refs[:count], refs[count:-1], refs[-1]):
        copy.wait()


def early_kernel(subs, reps, names, place_ref, weight_ref, *refs):
    outs = 2 + subs - 1 + 2
    refs, (u_ref, v_ref, *rest) = refs[: len(refs) - outs], refs[len(refs) - outs :]
    x_refs, (row_ref, col_ref) = rest[: subs - 1], rest[subs - 1 :]
    own, beside, refs = refs[0], refs[1:reps], refs[reps:]
    rows, cols = own.shape[2:]
    owned = own.shape[1]
    across = [refs[m * (subs - 1) : (m + 1) * (subs - 1)] for m in range(owned)]
    arrived = refs[owned * (subs - 1) :]
    for n in range(owned):
        for c in range(2):
            for i in range(reps):
                at = block(place_ref[1 + subs + i], cols)
                put_left(row_ref, n, c, at, (own if i == 0 else beside[i - 1])[c, n])
            for i in range(subs):
                matrix = own[c, n] if i == 0 else across[n][i - 1][c]
                put_right(col_ref, n, c, block(place_ref[1 + i], rows), matrix)
            nodes = [own[c, m] for m in range(owned)] + [a[c] for a in arrived]
            u_ref[n, c] = sum(weight_ref[n * names + k] * node for k, node in enumerate(nodes))
            v_ref[n, c] = sum(weight_ref[(owned + n) * names + k] * node for k, node in enumerate(nodes))
            for j in range(subs - 1):
                x_refs[j][n, c] = sum(weight_ref[n * names + m] * across[m][j][c] for m in range(owned))


def mix_kernel(row, names, first, fresh, slot_ref, weight_ref, v_ref, *refs):
    items, nodes, (item_ref, out_ref, sems) = refs[:fresh], refs[fresh:-3], refs[-3:]
    slot = jnp.max(slot_ref[row]).astype(jnp.int32)
    [copy] = copy_chosen([slot], nodes, [item_ref], sems)
    for n in range(v_ref.shape[0]):
        for c in range(2):
            v = v_ref[n, c]
            for k, item in enumerate(items):
                v = v + weight_ref[n * names + first + k] * item[c]
            out_ref[n, c] = v
    copy.wait()


def sum_kernel(subs, reps, names, gone, seen, arrived, place_ref, weight_ref, row_ref, col_ref, *refs):
    u, v, refs = refs[:subs], refs[subs : subs + reps], refs[subs + reps :]
    items, over, (out_ref, left_ref, v_parts, u_parts) = refs[:arrived], refs[arrived:-4], refs[-4:]
    rows, cols = out_ref.shape[2:]
    owned = out_ref.shape[0]
    for n in range(owned):
        for c in range(2):
            for i in range(subs):
                total = u[i][n, c]
                if i == 0:
                    for k, item in enumerate(items):
                        total = total + weight_ref[n * names + seen + k] * item[c]
                else:
                    for k, item in enumerate(over[i - 1 :: subs - 1]):
                        total = total + weight_ref[2 * owned * names + n * gone + k] * item[c]
                put_right(u_parts, n, c, block(place_ref[1 + i], rows), total)
            for i in range(reps):
                put_left(v_parts, n, c, block(place_ref[1 + subs + i], cols), v[i][n, c])
        one = product(row_ref[n], *right_parts(u_parts, n))
        two = product(v_parts[n], *right_parts(col_ref, n))
        out_ref[n, 0] = one[0] + two[0]
        out_ref[n, 1] = one[1] + two[1]
        for j in range(subs - 1):
            left_ref[j, n] = row_ref[n, :, :, :, block(place_ref[2 + j], rows)]


def late_kernel(subs, first, stride, weight_ref, sum_ref, left_ref, *refs):
    over, out_ref = refs[: subs - 1], refs[subs - 1]
    for n in range(sum_ref.shape[0]):
        real, imag = sum_ref[n, 0], sum_ref[n, 1]
        for j in range(subs - 1):
            one = product(left_ref[j, n], *[split(weight_ref[first + stride * n] * over[j][c]) for c in range(2)])
            real, imag = real + one[0], imag + one[1]
        out_ref[n, 0] = real
        out_ref[n, 1] = imag


def times_resident(cells, i, place_ref, pick_ref, col_ref, s_ref, n):
    at = block(place_ref[1 + cells + i], s_ref.shape[3])
    node = pick_ref[place_ref[0] * s_ref.shape[0] + n]
    parts = [split(s_ref[n, c]) for c in range(2)]
    left = jnp.stack([jnp.stack([parts[c][part] for c in range(2)]) for part in range(2)])
    return product(left, *[(col_ref[node, c, 0, at, :], col_ref[node, c, 1, at, :]) for c in range(2)])


def half_kernel(cells, place_ref, pick_ref, col_ref, s_ref, out_ref):
    for n in range(s_ref.shape[0]):
        out_ref[0, n], out_ref[1, n] = times_resident(cells, 0, place_ref, pick_ref, col_ref, s_ref, n)


def last_kernel(cells, place_ref, pick_ref, col_ref, half_ref, *refs):
    for n in range(half_ref.shape[1]):
        real, imag = half_ref[0, n], half_ref[1, n]
        for i, s_ref in enumerate(refs[:-1]):
            one = times_resident(cells, 1 + i, place_ref, pick_ref, col_ref, s_ref, n)
            real, imag = real + one[0], imag + one[1]
        refs[-1][0, n] = real
        refs[-1][1, n] = imag


def way_kernel(groups, fixed, *refs):
    lengths, out_ref = refs[:groups], refs[groups]
    way = jnp.int32(0)
    for length in lengths:
        way = jnp.maximum(way, jnp.maximum(length[0] - fixed, length[1] - fixed - 1))
    out_ref[0] = jnp.minimum(way, 2)


def call(kernel, scalars, arrays, outs, scratch=(), to=pltpu.VMEM):
    return pl.pallas_call(
        kernel,
        out_shape=outs,
        in_specs=[pl.BlockSpec(memory_space=pltpu.SMEM)] * len(scalars)
        + [pl.BlockSpec(memory_space=pltpu.VMEM)] * len(arrays),
        out_specs=jax.tree.map(lambda _: pl.BlockSpec(memory_space=to), outs),
        scratch_shapes=list(scratch),
        compiler_params=pltpu.CompilerParams(vmem_limit_bytes=VMEM_BYTES),
        cost_estimate=pl.CostEstimate(flops=1000, bytes_accessed=1000, transcendentals=0),
    )(*scalars, *arrays)


def shifts(array, axis):
    size = lax.axis_size(axis)
    return [lax.ppermute(array, axis, [(i, (i + j) % size) for i in range(size)]) for j in range(1, size)]


def places(axis):
    size = lax.axis_size(axis)
    return [(lax.axis_index(axis) - j) % size for j in range(size)]


def body(meson_nodes, term_nodes, weight_codes, resident_pick):
    line = lax.axis_size("node")
    subs, reps = lax.axis_size("sub"), lax.axis_size("rep")
    _, owned, rows, cols = meson_nodes.shape
    count = owned * line
    terms = term_nodes.shape[0]
    me = lax.axis_index("node")
    base = me * owned
    to_left = [(z + 1, z) for z in range(line - 1)]
    to_right = [(z, z + 1) for z in range(line - 1)]
    node_shape = (2, rows, cols)
    nodes_shape = (owned, 2, rows, cols)
    depth = rows * subs
    fixed = min(line - 1, UNROLLED)
    opened = fixed + 1

    def out(shape, dtype=jnp.float32):
        return jax.ShapeDtypeStruct(shape, dtype)

    def near(shape, dtype=jnp.float32):
        return pltpu.VMEM(shape, dtype)

    place = jnp.stack([me, *places("sub"), *places("rep")]).astype(jnp.int32)
    slots, weights, tables, length = plan_rounds(
        place, term_nodes.T, weight_codes, line, owned, round_bound(line, owned, terms), opened, cols
    )

    names = owned + 2 * opened
    gone = opened + 1 - FIRST_OVER
    pairs = [[(z, z + 1) for z in range(start, line - 1, 2)] for start in range(2)]
    swaps = [pair + [(j, i) for i, j in pair] for pair in pairs]

    def choose(step, kinds, came):
        nodes = [*own, *came]
        return pl.pallas_call(
            functools.partial(choose_kernel, [3 * step + kind for kind in kinds]),
            out_shape=[out(node_shape)] * len(kinds),
            in_specs=[pl.BlockSpec(memory_space=pltpu.VMEM)] + [pl.BlockSpec(memory_space=pl.ANY)] * len(nodes),
            out_specs=[pl.BlockSpec(memory_space=pltpu.VMEM)] * len(kinds),
            scratch_shapes=[pltpu.SemaphoreType.DMA((len(kinds),))],
            compiler_params=pltpu.CompilerParams(vmem_limit_bytes=VMEM_BYTES),
            cost_estimate=pl.CostEstimate(flops=1000, bytes_accessed=1000, transcendentals=0),
        )(slots, *nodes)

    def meet(first, second):
        return [lax.ppermute(item, "node", swap) for item, swap in zip((first, second), swaps)]

    first, second, *own = pl.pallas_call(
        functools.partial(first_kernel, line, owned, terms),
        out_shape=[out(node_shape)] * (2 + owned),
        in_specs=[pl.BlockSpec(memory_space=space) for space in (pltpu.SMEM, pl.ANY, pl.ANY)],
        out_specs=[pl.BlockSpec(memory_space=pltpu.VMEM)] * (2 + owned),
        scratch_shapes=[
            pltpu.SMEM(term_nodes.shape[::-1], jnp.int32),
            pltpu.SemaphoreType.DMA,
            pltpu.SemaphoreType.DMA((2, owned)),
        ],
        compiler_params=pltpu.CompilerParams(vmem_limit_bytes=VMEM_BYTES),
        cost_estimate=pl.CostEstimate(flops=1000, bytes_accessed=1000, transcendentals=0),
    )(place, term_nodes.T, meson_nodes)
    came, across, over = [], [], []
    lengths = [length, *shifts(length, "grp")]
    for step in range(fixed):
        if step < FIRST_OVER:
            beyond = own[step : owned if step == FIRST_OVER - 1 else step + 1]
            if step > 0:
                first, second = choose(step, (0, 1), came)
        else:
            first, second, *beyond = choose(step, (0, 1, 2), came)
        beyond = [x for item in beyond for x in shifts(item, "sub")]
        new, beyond = lax.optimization_barrier((meet(first, second), beyond))
        came = came + new
        if step < FIRST_OVER:
            across = across + beyond
        else:
            over = over + beyond
        if step == FIRST_OVER - 1:
            beside = shifts(meson_nodes, "rep")
            came, beside, lengths = lax.optimization_barrier((came, beside, lengths))
            before = len(came)
            way = pl.pallas_call(
                functools.partial(way_kernel, len(lengths), fixed),
                out_shape=jax.ShapeDtypeStruct((1,), jnp.int32),
                in_specs=[pl.BlockSpec(memory_space=pltpu.SMEM)] * len(lengths),
                out_specs=pl.BlockSpec(memory_space=pltpu.SMEM),
            )(*lengths)

    row_part, col_part = (owned, 2, 2, rows, depth), (owned, 2, 2, depth, cols)

    def begin(beside, across, came):
        *mixed, row, col = call(
            functools.partial(early_kernel, subs, reps, names),
            [place],
            [weights, meson_nodes, *beside, *across, *came],
            [out(nodes_shape), near(nodes_shape)]
            + [out(nodes_shape)] * (subs - 1)
            + [out(row_part, jnp.bfloat16), out(col_part, jnp.bfloat16)],
        )
        return mixed, row, col

    early, row, col = begin(beside, across, came[:before])

    def sums(row, col, u, v, items=(), over=()):
        return call(
            functools.partial(sum_kernel, subs, reps, names, gone, owned + before, len(items)),
            [place],
            [weights, row, col, *u, v, *shifts(v, "rep"), *items, *over],
            [out(nodes_shape), out((subs - 1, owned, 2, 2, rows, rows), jnp.bfloat16)],
            [pltpu.VMEM(row_part, jnp.bfloat16), pltpu.VMEM(col_part, jnp.bfloat16)],
        )

    def end(step, came, over):
        u, v, *ux = early
        fresh, nodes = came[before:], [*own, *came]
        item, v = pl.pallas_call(
            functools.partial(mix_kernel, 3 * step + 2, names, owned * names + owned + before, len(fresh)),
            out_shape=[out(node_shape), out(nodes_shape)],
            in_specs=[pl.BlockSpec(memory_space=pltpu.VMEM)] * (3 + len(fresh))
            + [pl.BlockSpec(memory_space=pl.ANY)] * len(nodes),
            out_specs=[pl.BlockSpec(memory_space=pltpu.VMEM)] * 2,
            scratch_shapes=[pltpu.SemaphoreType.DMA((1,))],
            compiler_params=pltpu.CompilerParams(vmem_limit_bytes=VMEM_BYTES),
            cost_estimate=pl.CostEstimate(flops=1000, bytes_accessed=1000, transcendentals=0),
        )(slots, weights, v, *fresh, *nodes)
        late = shifts(item, "sub")
        first = 2 * owned * names + step - FIRST_OVER
        return call(
            functools.partial(late_kernel, subs, first, gone),
            [],
            [weights, *sums(row, col, [u, *ux], v, fresh, over), *late],
            out(nodes_shape),
        )

    def short(_):
        return end(fixed, came, over)

    def middle(_):
        first, second, item = choose(fixed, (0, 1, 2), came)
        new, beyond = lax.optimization_barrier((meet(first, second), shifts(item, "sub")))
        return end(fixed + 1, came + new, over + beyond)

    def long(_):
        edges = jnp.pad(tables.reshape(-1, 3, line), ((0, 0), (0, 0), (1, 1)), constant_values=count)
        mine = lax.dynamic_slice_in_dim(edges, me, 3, axis=2)
        rounds = functools.reduce(jnp.maximum, [length[1] for length in lengths])
        leading, trailing = term_nodes[:, 0], term_nodes[:, 1]
        factors = (weight_codes.astype(jnp.float32) - 3.5) * 0.5
        mine_ids = base + jnp.arange(owned, dtype=jnp.int32)
        first_mine = factors[:, None] * (leading[:, None] == mine_ids)
        second_mine = factors[:, None] * (trailing[:, None] == mine_ids)
        held = jnp.zeros((count + 1, 2, rows, cols), jnp.float32)
        held = lax.dynamic_update_slice(held, jnp.swapaxes(meson_nodes, 0, 1), (base, 0, 0, 0))
        across = [x for m in range(owned) for x in shifts(meson_nodes[:, m], "sub")]
        (u, v, *ux), row, col = begin(shifts(meson_nodes, "rep"), across, [])

        def add(total, mine_terms, others, name, item):
            scale = jnp.sum(mine_terms * (others == name)[:, None], axis=0)
            return total + scale[:, None, None, None] * item[None]

        def more(state):
            return state[0] < rounds

        def again(state):
            step, held, u, v = state
            ids = lax.dynamic_index_in_dim(mine, step, 0, keepdims=False)
            left, right, item = lax.optimization_barrier(
                tuple(lax.dynamic_index_in_dim(held, ids[i, 1], 0, keepdims=False) for i in range(3))
            )
            from_right = lax.ppermute(left, "node", to_left)
            from_left = lax.ppermute(right, "node", to_right)
            items = [item, *shifts(item, "sub")]
            from_right, from_left = lax.optimization_barrier((from_right, from_left))
            u = [add(total, first_mine, trailing, ids[2, 1], x) for total, x in zip(u, items)]
            v = add(v, second_mine, leading, ids[0, 2], from_right)
            v = add(v, second_mine, leading, ids[1, 0], from_left)
            held = lax.dynamic_update_slice_in_dim(held, from_right[None], ids[0, 2], 0)
            held = lax.dynamic_update_slice_in_dim(held, from_left[None], ids[1, 0], 0)
            return step + 1, held, u, v

        _, _, u, v = lax.while_loop(more, again, (jnp.int32(0), held, [u, *ux], v))
        return sums(row, col, u, v)[0]

    summed = lax.switch(way[0], [short, middle, long], None)
    half = call(functools.partial(half_kernel, subs), [place, resident_pick], [col, summed], out(meson_nodes.shape))
    return call(
        functools.partial(last_kernel, subs),
        [place, resident_pick],
        [col, half, *shifts(summed, "rep")],
        out(meson_nodes.shape),
    )


def solution(mesh):
    in_specs = (P(None, ("grp", "node"), "sub", "rep"), P("grp", None), P("grp"), P("grp"))
    out_specs = P(None, ("grp", "node"), "sub", "rep")
    return jax.shard_map(body, mesh=mesh, in_specs=in_specs, out_specs=out_specs, check_vma=False)
```

```python
import functools

import jax
import jax.numpy as jnp
from jax import lax
from jax.experimental import pallas as pl
from jax.experimental.pallas import tpu as pltpu
from jax.sharding import PartitionSpec as P

VMEM_BYTES = 20 * 2**20
UNROLLED = 3
FIRST_OVER = 2


def round_bound(line, owned, terms):
    most = min(terms, owned)
    for hop in range(2, line):
        most = max(min(terms, owned * hop), most + 1)
    return max(most, FIRST_OVER) + terms


def plan_kernel(line, owned, terms, rounds, opened, *refs):
    place_ref, all_terms_ref, codes_ref, slot_ref, weight_ref, table_ref, length_ref, terms_ref, sem = refs
    fetch(all_terms_ref, terms_ref, sem)
    count = line * owned
    shape = (line, count)
    ids = lax.broadcasted_iota(jnp.int32, shape, 1)
    place = lax.broadcasted_iota(jnp.int32, shape, 0)
    home = ids // owned
    lowest, highest = home, home
    wanted = jnp.zeros(shape, jnp.float32)
    me = place_ref[0]
    even = lax.rem(me, 2) == 0
    pairs = [(terms_ref[0, t], terms_ref[1, t]) for t in range(terms)]
    for a, b in pairs:
        first_home, second_home = a // owned, b // owned
        other = jnp.where(ids == a, second_home, jnp.where(ids == b, first_home, home))
        lowest = jnp.minimum(lowest, other)
        highest = jnp.maximum(highest, other)
        wanted = jnp.where((place == first_home) & (ids == b) & (home != place), 1.0, wanted)

    def pick(score):
        best = jnp.max(score, axis=1, keepdims=True)
        chosen = jnp.where((score == best) & (score > 0.0), 1.0, 0.0)
        return best, chosen, jnp.sum(chosen * (ids - count).astype(jnp.float32), axis=1, keepdims=True) + float(count)

    def anywhere(chosen):
        return jnp.max(chosen, axis=0, keepdims=True).astype(jnp.int32)

    rank = lax.broadcasted_iota(jnp.int32, (line, 1), 0)

    def of(send, who):
        return jnp.sum(jnp.where(rank == who, send - float(count), 0.0), axis=0, keepdims=True).astype(jnp.int32) + count

    names = [jnp.full((1, 1), me * owned + m, jnp.int32) for m in range(owned)]

    def write(row, send):
        wanted_name = of(send, me)
        slot = jnp.zeros((1, 1), jnp.float32)
        for k, name in enumerate(names):
            slot = jnp.where(wanted_name == name, float(k), slot)
        slot_ref[row] = jnp.broadcast_to(slot, slot_ref.shape[1:])
        return wanted_name

    left, right = home, home
    lane = lax.broadcasted_iota(jnp.int32, (line, 2), 1)
    length = jnp.zeros((line, 2), jnp.int32)
    gone = []
    for step in range(rounds):
        to_go = jnp.where((left == place) & (lowest < place), place - lowest, 0)
        best_left, moved_left, send_left = pick(jnp.where(to_go > 0, (to_go + 1) * count - ids, 0).astype(jnp.float32))
        to_go = jnp.where((right == place) & (highest > place), highest - place, 0)
        best_right, moved_right, send_right = pick(jnp.where(to_go > 0, (to_go + 1) * count - ids, 0).astype(jnp.float32))
        busy_line = jnp.max(jnp.maximum(best_left, best_right), axis=0, keepdims=True)
        if step >= FIRST_OVER:
            here = ((left <= place) & (place < home)) | ((right >= place) & (place > home))
            best_over, moved_over, send_over = pick(jnp.where(here, wanted * (count - ids).astype(jnp.float32), 0.0))
            wanted = wanted - moved_over
            busy = jnp.maximum(busy_line, jnp.max(best_over, axis=0, keepdims=True))
        else:
            send_over, busy = jnp.full((line, 1), float(count), jnp.float32), busy_line
        for i, send in enumerate((send_left, send_right, send_over)):
            table_ref[3 * step + i] = send.astype(jnp.int32)
        if step <= opened:
            first = jnp.where(even, send_right, send_left)
            second = jnp.where(even, send_left, send_right)
            for i, send in enumerate((first, second, send_over)):
                name = write(3 * step + i, send)
                if i == 2 and step >= FIRST_OVER:
                    gone.append(name)
            come_left, come_right = of(send_left, me + 1), of(send_right, me - 1)
            names += [jnp.where(even, come_left, come_right), jnp.where(even, come_right, come_left)]
        left = left - anywhere(moved_left)
        right = right + anywhere(moved_right)
        length = jnp.where(jnp.where(lane == 0, busy_line, busy) > 0.0, step + 1, length)
    length_ref[0] = jnp.max(length[:, :1].astype(jnp.float32)).astype(jnp.int32)
    length_ref[1] = jnp.max(length[:, 1:].astype(jnp.float32)).astype(jnp.int32)

    names = names[: owned + 2 * opened]
    row = 0
    for side, queue in ((0, names), (1, names), (0, gone)):
        for n in range(owned):
            scales = [
                jnp.where(ours[side] == me * owned + n, (codes_ref[t].astype(jnp.float32) - 3.5) * 0.5, 0.0)
                for t, ours in enumerate(pairs)
            ]
            for name in queue:
                weight = jnp.zeros((1, 1), jnp.float32)
                for scale, ours in zip(scales, pairs):
                    weight = weight + jnp.where(name == ours[1 - side], scale, 0.0)
                weight_ref[row] = jnp.broadcast_to(weight, weight_ref.shape[1:])
                row += 1


def plan_rounds(me, term_nodes, weight_codes, line, owned, rounds, opened, cols):
    overs = opened + 1 - FIRST_OVER
    rows = owned * (2 * (owned + 2 * opened) + overs)
    slots, weights, tables, lengths = pl.pallas_call(
        functools.partial(plan_kernel, line, owned, term_nodes.shape[1], rounds, opened),
        out_shape=[
            jax.ShapeDtypeStruct((3 * (opened + 1), 1, 128), jnp.float32),
            jax.ShapeDtypeStruct((rows, 1, cols), jnp.float32),
            jax.ShapeDtypeStruct((3 * rounds, line, 1), jnp.int32),
            jax.ShapeDtypeStruct((2,), jnp.int32),
        ],
        in_specs=[pl.BlockSpec(memory_space=space) for space in (pltpu.SMEM, pl.ANY, pltpu.SMEM)],
        scratch_shapes=[pltpu.SMEM(term_nodes.shape, jnp.int32), pltpu.SemaphoreType.DMA],
        out_specs=[pl.BlockSpec(memory_space=pltpu.VMEM)] * 3 + [pl.BlockSpec(memory_space=pltpu.SMEM)],
        cost_estimate=pl.CostEstimate(flops=1000, bytes_accessed=1000, transcendentals=0),
    )(me, term_nodes, weight_codes)
    return slots, weights, tables, lengths


def split(value):
    high = value.astype(jnp.bfloat16)
    return high, (value - high.astype(jnp.float32)).astype(jnp.bfloat16)


def product(left, right_real, right_imag):
    rows = left.shape[2]
    every = left.reshape(4 * rows, left.shape[3])
    dot = functools.partial(jnp.dot, preferred_element_type=jnp.float32)

    def times(high, low):
        one, two = dot(every, high), dot(every[: 2 * rows], low)
        both = one[: 2 * rows] + (one[2 * rows :] + two)
        return both[:rows], both[rows:]

    real_real, imag_real = times(*right_real)
    real_imag, imag_imag = times(*right_imag)
    return real_real - imag_imag, real_imag + imag_real


def put_left(ref, n, c, cols, value):
    for part, piece in enumerate(split(value)):
        ref[n, part, c, :, cols] = piece


def put_right(ref, n, c, rows, value):
    for part, piece in enumerate(split(value)):
        ref[n, c, part, rows, :] = piece


def right_parts(ref, n):
    return [(ref[n, c, 0], ref[n, c, 1]) for c in range(2)]


def block(index, size):
    return pl.ds(pl.multiple_of(index * size, size), size)


def fetch(terms_ref, terms_here, sem):
    copy = pltpu.make_async_copy(terms_ref, terms_here, sem)
    copy.start()
    copy.wait()


def copy_chosen(slots, nodes, outs, sems):
    for i, (slot, out_ref) in enumerate(zip(slots, outs)):
        for k, node in enumerate(nodes):

            @pl.when(slot == k)
            def _(node=node, out_ref=out_ref, i=i):
                pltpu.make_async_copy(node, out_ref, sems.at[i]).start()

    return [pltpu.make_async_copy(nodes[0], out_ref, sems.at[i]) for i, out_ref in enumerate(outs)]


def first_kernel(line, owned, terms, place_ref, terms_ref, own_ref, first_ref, second_ref, *refs):
    copies, (terms_here, sem, sems) = refs[:owned], refs[owned:]
    moves = [
        pltpu.make_async_copy(own_ref.at[c, m], copies[m].at[c], sems.at[c, m]) for m in range(owned) for c in range(2)
    ]
    fetch = pltpu.make_async_copy(terms_ref, terms_here, sem)
    for move in [fetch, *moves]:
        move.start()
    fetch.wait()
    me = place_ref[0]
    choice = []
    lows, highs = [jnp.int32(0)] * owned, [jnp.int32(0)] * owned
    for t in range(terms):
        a, b = terms_here[0, t], terms_here[1, t]
        to_second, to_first = b // owned - me, a // owned - me
        for m in range(owned):
            name = me * owned + m
            away = jnp.where(a == name, to_second, jnp.where(b == name, to_first, 0))
            lows[m] = jnp.maximum(lows[m], -away)
            highs[m] = jnp.maximum(highs[m], away)
    for far in (lows, highs):
        best, slot = far[0], jnp.int32(0)
        for m in range(1, owned):
            slot = jnp.where(far[m] > best, m, slot)
            best = jnp.maximum(far[m], best)
        choice.append(slot)
    even = lax.rem(me, 2) == 0
    slots = (jnp.where(even, choice[1], choice[0]), jnp.where(even, choice[0], choice[1]))
    for move in moves:
        move.wait()
    for slot, out_ref in zip(slots, (first_ref, second_ref)):
        for m in range(owned):

            @pl.when(slot == m)
            def _(m=m, out_ref=out_ref):
                out_ref[...] = copies[m][...]


def choose_kernel(rows, slot_ref, *refs):
    count = len(refs) - 1 - len(rows)
    slots = [jnp.max(slot_ref[row]).astype(jnp.int32) for row in rows]
    for copy in copy_chosen(slots, refs[:count], refs[count:-1], refs[-1]):
        copy.wait()


def early_kernel(subs, reps, names, place_ref, weight_ref, *refs):
    outs = 2 + subs - 1 + 2
    refs, (u_ref, v_ref, *rest) = refs[: len(refs) - outs], refs[len(refs) - outs :]
    x_refs, (row_ref, col_ref) = rest[: subs - 1], rest[subs - 1 :]
    own, beside, refs = refs[0], refs[1:reps], refs[reps:]
    rows, cols = own.shape[2:]
    owned = own.shape[1]
    across = [refs[m * (subs - 1) : (m + 1) * (subs - 1)] for m in range(owned)]
    arrived = refs[owned * (subs - 1) :]
    for n in range(owned):
        for c in range(2):
            for i in range(reps):
                at = block(place_ref[1 + subs + i], cols)
                put_left(row_ref, n, c, at, (own if i == 0 else beside[i - 1])[c, n])
            for i in range(subs):
                matrix = own[c, n] if i == 0 else across[n][i - 1][c]
                put_right(col_ref, n, c, block(place_ref[1 + i], rows), matrix)
            nodes = [own[c, m] for m in range(owned)] + [a[c] for a in arrived]
            u_ref[n, c] = sum(weight_ref[n * names + k] * node for k, node in enumerate(nodes))
            v_ref[n, c] = sum(weight_ref[(owned + n) * names + k] * node for k, node in enumerate(nodes))
            for j in range(subs - 1):
                x_refs[j][n, c] = sum(weight_ref[n * names + m] * across[m][j][c] for m in range(owned))


def sum_kernel(subs, reps, names, gone, seen, arrived, place_ref, weight_ref, row_ref, col_ref, *refs):
    u, v, refs = refs[:subs], refs[subs : subs + reps], refs[subs + reps :]
    came = [refs[i * arrived : (i + 1) * arrived] for i in range(reps)]
    items, over, (out_ref, left_ref, v_parts, u_parts) = came[0], refs[reps * arrived : -4], refs[-4:]
    rows, cols = out_ref.shape[2:]
    owned = out_ref.shape[0]
    for n in range(owned):
        for c in range(2):
            for i in range(subs):
                total = u[i][n, c]
                if i == 0:
                    for k, item in enumerate(items):
                        total = total + weight_ref[n * names + seen + k] * item[c]
                else:
                    for k, item in enumerate(over[i - 1 :: subs - 1]):
                        total = total + weight_ref[2 * owned * names + n * gone + k] * item[c]
                put_right(u_parts, n, c, block(place_ref[1 + i], rows), total)
            for i in range(reps):
                total = v[i][n, c]
                for k, item in enumerate(came[i]):
                    total = total + weight_ref[(owned + n) * names + seen + k] * item[c]
                put_left(v_parts, n, c, block(place_ref[1 + subs + i], cols), total)
        one = product(row_ref[n], *right_parts(u_parts, n))
        two = product(v_parts[n], *right_parts(col_ref, n))
        out_ref[n, 0] = one[0] + two[0]
        out_ref[n, 1] = one[1] + two[1]
        for j in range(subs - 1):
            left_ref[j, n] = row_ref[n, :, :, :, block(place_ref[2 + j], rows)]


def late_kernel(subs, first, stride, weight_ref, sum_ref, left_ref, *refs):
    over, out_ref = refs[: subs - 1], refs[subs - 1]
    for n in range(sum_ref.shape[0]):
        real, imag = sum_ref[n, 0], sum_ref[n, 1]
        for j in range(subs - 1):
            one = product(left_ref[j, n], *[split(weight_ref[first + stride * n] * over[j][c]) for c in range(2)])
            real, imag = real + one[0], imag + one[1]
        out_ref[n, 0] = real
        out_ref[n, 1] = imag


def times_resident(cells, i, place_ref, pick_ref, col_ref, s_ref, n):
    at = block(place_ref[1 + cells + i], s_ref.shape[3])
    node = pick_ref[place_ref[0] * s_ref.shape[0] + n]
    parts = [split(s_ref[n, c]) for c in range(2)]
    left = jnp.stack([jnp.stack([parts[c][part] for c in range(2)]) for part in range(2)])
    return product(left, *[(col_ref[node, c, 0, at, :], col_ref[node, c, 1, at, :]) for c in range(2)])


def half_kernel(cells, place_ref, pick_ref, col_ref, s_ref, out_ref):
    for n in range(s_ref.shape[0]):
        out_ref[0, n], out_ref[1, n] = times_resident(cells, 0, place_ref, pick_ref, col_ref, s_ref, n)


def last_kernel(cells, place_ref, pick_ref, col_ref, half_ref, *refs):
    for n in range(half_ref.shape[1]):
        real, imag = half_ref[0, n], half_ref[1, n]
        for i, s_ref in enumerate(refs[:-1]):
            one = times_resident(cells, 1 + i, place_ref, pick_ref, col_ref, s_ref, n)
            real, imag = real + one[0], imag + one[1]
        refs[-1][0, n] = real
        refs[-1][1, n] = imag


def way_kernel(groups, fixed, *refs):
    lengths, out_ref = refs[:groups], refs[groups]
    way = jnp.int32(0)
    for length in lengths:
        way = jnp.maximum(way, jnp.maximum(length[0] - fixed, length[1] - fixed - 1))
    out_ref[0] = jnp.minimum(way, 2)


def call(kernel, scalars, arrays, outs, scratch=()):
    return pl.pallas_call(
        kernel,
        out_shape=outs,
        in_specs=[pl.BlockSpec(memory_space=pltpu.SMEM)] * len(scalars)
        + [pl.BlockSpec(memory_space=pltpu.VMEM)] * len(arrays),
        out_specs=jax.tree.map(lambda _: pl.BlockSpec(memory_space=pltpu.VMEM), outs),
        scratch_shapes=list(scratch),
        compiler_params=pltpu.CompilerParams(vmem_limit_bytes=VMEM_BYTES),
        cost_estimate=pl.CostEstimate(flops=1000, bytes_accessed=1000, transcendentals=0),
    )(*scalars, *arrays)


def shifts(array, axis):
    size = lax.axis_size(axis)
    return [lax.ppermute(array, axis, [(i, (i + j) % size) for i in range(size)]) for j in range(1, size)]


def places(axis):
    size = lax.axis_size(axis)
    return [(lax.axis_index(axis) - j) % size for j in range(size)]


def body(meson_nodes, term_nodes, weight_codes, resident_pick):
    line = lax.axis_size("node")
    subs, reps = lax.axis_size("sub"), lax.axis_size("rep")
    _, owned, rows, cols = meson_nodes.shape
    count = owned * line
    terms = term_nodes.shape[0]
    me = lax.axis_index("node")
    base = me * owned
    to_left = [(z + 1, z) for z in range(line - 1)]
    to_right = [(z, z + 1) for z in range(line - 1)]
    node_shape = (2, rows, cols)
    nodes_shape = (owned, 2, rows, cols)
    depth = rows * subs
    fixed = min(line - 1, UNROLLED)
    opened = fixed + 1

    def out(shape, dtype=jnp.float32):
        return jax.ShapeDtypeStruct(shape, dtype)

    def near(shape, dtype=jnp.float32):
        return pltpu.VMEM(shape, dtype)

    place = jnp.stack([me, *places("sub"), *places("rep")]).astype(jnp.int32)
    slots, weights, tables, length = plan_rounds(
        place, term_nodes.T, weight_codes, line, owned, round_bound(line, owned, terms), opened, cols
    )

    names = owned + 2 * opened
    gone = opened + 1 - FIRST_OVER
    pairs = [[(z, z + 1) for z in range(start, line - 1, 2)] for start in range(2)]
    swaps = [pair + [(j, i) for i, j in pair] for pair in pairs]

    def choose(step, kinds, came):
        nodes = [*own, *came]
        return pl.pallas_call(
            functools.partial(choose_kernel, [3 * step + kind for kind in kinds]),
            out_shape=[out(node_shape)] * len(kinds),
            in_specs=[pl.BlockSpec(memory_space=pltpu.VMEM)] + [pl.BlockSpec(memory_space=pl.ANY)] * len(nodes),
            out_specs=[pl.BlockSpec(memory_space=pltpu.VMEM)] * len(kinds),
            scratch_shapes=[pltpu.SemaphoreType.DMA((len(kinds),))],
            compiler_params=pltpu.CompilerParams(vmem_limit_bytes=VMEM_BYTES),
            cost_estimate=pl.CostEstimate(flops=1000, bytes_accessed=1000, transcendentals=0),
        )(slots, *nodes)

    def meet(first, second):
        return [lax.ppermute(item, "node", swap) for item, swap in zip((first, second), swaps)]

    first, second, *own = pl.pallas_call(
        functools.partial(first_kernel, line, owned, terms),
        out_shape=[out(node_shape)] * (2 + owned),
        in_specs=[pl.BlockSpec(memory_space=space) for space in (pltpu.SMEM, pl.ANY, pl.ANY)],
        out_specs=[pl.BlockSpec(memory_space=pltpu.VMEM)] * (2 + owned),
        scratch_shapes=[
            pltpu.SMEM(term_nodes.shape[::-1], jnp.int32),
            pltpu.SemaphoreType.DMA,
            pltpu.SemaphoreType.DMA((2, owned)),
        ],
        compiler_params=pltpu.CompilerParams(vmem_limit_bytes=VMEM_BYTES),
        cost_estimate=pl.CostEstimate(flops=1000, bytes_accessed=1000, transcendentals=0),
    )(place, term_nodes.T, meson_nodes)
    came, across, over = [], [], []
    lengths = [length, *shifts(length, "grp")]
    for step in range(fixed):
        if step < FIRST_OVER:
            beyond = own[step : owned if step == FIRST_OVER - 1 else step + 1]
            if step > 0:
                first, second = choose(step, (0, 1), came)
        else:
            first, second, *beyond = choose(step, (0, 1, 2), came)
        beyond = [x for item in beyond for x in shifts(item, "sub")]
        new, beyond = lax.optimization_barrier((meet(first, second), beyond))
        came = came + new
        if step < FIRST_OVER:
            across = across + beyond
        else:
            over = over + beyond
        if step == FIRST_OVER - 1:
            beside = shifts(meson_nodes, "rep")
            came, beside, lengths = lax.optimization_barrier((came, beside, lengths))
            before = len(came)
            way = pl.pallas_call(
                functools.partial(way_kernel, len(lengths), fixed),
                out_shape=jax.ShapeDtypeStruct((1,), jnp.int32),
                in_specs=[pl.BlockSpec(memory_space=pltpu.SMEM)] * len(lengths),
                out_specs=pl.BlockSpec(memory_space=pltpu.SMEM),
            )(*lengths)

    row_part, col_part = (owned, 2, 2, rows, depth), (owned, 2, 2, depth, cols)

    def begin(beside, across, came):
        *mixed, row, col = call(
            functools.partial(early_kernel, subs, reps, names),
            [place],
            [weights, meson_nodes, *beside, *across, *came],
            [out(nodes_shape), near(nodes_shape)]
            + [out(nodes_shape)] * (subs - 1)
            + [out(row_part, jnp.bfloat16), out(col_part, jnp.bfloat16)],
        )
        return mixed, row, col

    early, row, col = begin(beside, across, came[:before])

    def sums(row, col, u, v, items=(), over=()):
        return call(
            functools.partial(sum_kernel, subs, reps, names, gone, owned + before, len(items) // reps),
            [place],
            [weights, row, col, *u, *v, *items, *over],
            [out(nodes_shape), out((subs - 1, owned, 2, 2, rows, rows), jnp.bfloat16)],
            [pltpu.VMEM(row_part, jnp.bfloat16), pltpu.VMEM(col_part, jnp.bfloat16)],
        )

    def beyond_rep(items):
        there = [shifts(item, "rep") for item in items]
        return [*items, *[each[j] for j in range(reps - 1) for each in there]]

    u, *ux = early[:1] + early[2:]

    def end(step, came, over):
        [item] = choose(step, (2,), came)
        late = shifts(item, "sub")
        fresh = beyond_rep(came[before:])
        v = [early[1], *shifts(early[1], "rep")]
        first = 2 * owned * names + step - FIRST_OVER
        return call(
            functools.partial(late_kernel, subs, first, gone),
            [],
            [weights, *sums(row, col, [u, *ux], v, fresh, over), *late],
            out(nodes_shape),
        )

    def short(_):
        return end(fixed, came, over)

    def middle(_):
        first, second, item = choose(fixed, (0, 1, 2), came)
        new, beyond = lax.optimization_barrier((meet(first, second), shifts(item, "sub")))
        return end(fixed + 1, came + new, over + beyond)

    def long(_):
        edges = jnp.pad(tables.reshape(-1, 3, line), ((0, 0), (0, 0), (1, 1)), constant_values=count)
        mine = lax.dynamic_slice_in_dim(edges, me, 3, axis=2)
        rounds = functools.reduce(jnp.maximum, [length[1] for length in lengths])
        leading, trailing = term_nodes[:, 0], term_nodes[:, 1]
        factors = (weight_codes.astype(jnp.float32) - 3.5) * 0.5
        mine_ids = base + jnp.arange(owned, dtype=jnp.int32)
        first_mine = factors[:, None] * (leading[:, None] == mine_ids)
        second_mine = factors[:, None] * (trailing[:, None] == mine_ids)
        held = jnp.zeros((count + 1, 2, rows, cols), jnp.float32)
        held = lax.dynamic_update_slice(held, jnp.swapaxes(meson_nodes, 0, 1), (base, 0, 0, 0))
        across = [x for m in range(owned) for x in shifts(meson_nodes[:, m], "sub")]
        (u, v, *ux), row, col = begin(shifts(meson_nodes, "rep"), across, [])

        def add(total, mine_terms, others, name, item):
            scale = jnp.sum(mine_terms * (others == name)[:, None], axis=0)
            return total + scale[:, None, None, None] * item[None]

        def more(state):
            return state[0] < rounds

        def again(state):
            step, held, u, v = state
            ids = lax.dynamic_index_in_dim(mine, step, 0, keepdims=False)
            left, right, item = lax.optimization_barrier(
                tuple(lax.dynamic_index_in_dim(held, ids[i, 1], 0, keepdims=False) for i in range(3))
            )
            from_right = lax.ppermute(left, "node", to_left)
            from_left = lax.ppermute(right, "node", to_right)
            items = [item, *shifts(item, "sub")]
            from_right, from_left = lax.optimization_barrier((from_right, from_left))
            u = [add(total, first_mine, trailing, ids[2, 1], x) for total, x in zip(u, items)]
            v = add(v, second_mine, leading, ids[0, 2], from_right)
            v = add(v, second_mine, leading, ids[1, 0], from_left)
            held = lax.dynamic_update_slice_in_dim(held, from_right[None], ids[0, 2], 0)
            held = lax.dynamic_update_slice_in_dim(held, from_left[None], ids[1, 0], 0)
            return step + 1, held, u, v

        _, _, u, v = lax.while_loop(more, again, (jnp.int32(0), held, [u, *ux], v))
        return sums(row, col, u, [v, *shifts(v, "rep")])[0]

    summed = lax.switch(way[0], [short, middle, long], None)
    half = call(functools.partial(half_kernel, subs), [place, resident_pick], [col, summed], out(meson_nodes.shape))
    return call(
        functools.partial(last_kernel, subs),
        [place, resident_pick],
        [col, half, *shifts(summed, "rep")],
        out(meson_nodes.shape),
    )


def solution(mesh):
    in_specs = (P(None, ("grp", "node"), "sub", "rep"), P("grp", None), P("grp"), P("grp"))
    out_specs = P(None, ("grp", "node"), "sub", "rep")
    return jax.shard_map(body, mesh=mesh, in_specs=in_specs, out_specs=out_specs, check_vma=False)
```

```python
import functools

import jax
import jax.numpy as jnp
from jax import lax
from jax.experimental import pallas as pl
from jax.experimental.pallas import tpu as pltpu
from jax.sharding import PartitionSpec as P

VMEM_BYTES = 20 * 2**20
UNROLLED = 3
FIRST_OVER = 2


def round_bound(line, owned, terms):
    most = min(terms, owned)
    for hop in range(2, line):
        most = max(min(terms, owned * hop), most + 1)
    return max(most, FIRST_OVER) + terms


def plan_kernel(line, owned, terms, rounds, opened, *refs):
    place_ref, all_terms_ref, codes_ref, slot_ref, weight_ref, table_ref, length_ref, terms_ref, sem = refs
    fetch(all_terms_ref, terms_ref, sem)
    count = line * owned
    shape = (line, count)
    ids = lax.broadcasted_iota(jnp.int32, shape, 1)
    place = lax.broadcasted_iota(jnp.int32, shape, 0)
    home = ids // owned
    lowest, highest = home, home
    wanted = jnp.zeros(shape, jnp.float32)
    me = place_ref[0]
    even = lax.rem(me, 2) == 0
    pairs = [(terms_ref[0, t], terms_ref[1, t]) for t in range(terms)]
    for a, b in pairs:
        first_home, second_home = a // owned, b // owned
        other = jnp.where(ids == a, second_home, jnp.where(ids == b, first_home, home))
        lowest = jnp.minimum(lowest, other)
        highest = jnp.maximum(highest, other)
        wanted = jnp.where((place == first_home) & (ids == b) & (home != place), 1.0, wanted)

    def pick(score):
        best = jnp.max(score, axis=1, keepdims=True)
        chosen = jnp.where((score == best) & (score > 0.0), 1.0, 0.0)
        return best, chosen, jnp.sum(chosen * (ids - count).astype(jnp.float32), axis=1, keepdims=True) + float(count)

    def anywhere(chosen):
        return jnp.max(chosen, axis=0, keepdims=True).astype(jnp.int32)

    rank = lax.broadcasted_iota(jnp.int32, (line, 1), 0)

    def of(send, who):
        return jnp.sum(jnp.where(rank == who, send - float(count), 0.0), axis=0, keepdims=True).astype(jnp.int32) + count

    names = [jnp.full((1, 1), me * owned + m, jnp.int32) for m in range(owned)]

    def write(row, send):
        wanted_name = of(send, me)
        slot = jnp.zeros((1, 1), jnp.float32)
        for k, name in enumerate(names):
            slot = jnp.where(wanted_name == name, float(k), slot)
        slot_ref[row] = jnp.broadcast_to(slot, slot_ref.shape[1:])
        return wanted_name

    def second_for(side):
        return jnp.max(jnp.where(side, wanted, 0.0), axis=0, keepdims=True).astype(jnp.int32)

    left_second, right_second = second_for(place < home), second_for(place > home)
    left, right = home, home
    lane = lax.broadcasted_iota(jnp.int32, (line, 2), 1)
    length = jnp.zeros((line, 2), jnp.int32)
    gone = []
    for step in range(rounds):
        to_go = jnp.where((left == place) & (lowest < place), place - lowest, 0)
        score = jnp.where(to_go > 0, (2 * to_go + left_second + 1) * count - ids, 0)
        best_left, moved_left, send_left = pick(score.astype(jnp.float32))
        to_go = jnp.where((right == place) & (highest > place), highest - place, 0)
        score = jnp.where(to_go > 0, (2 * to_go + right_second + 1) * count - ids, 0)
        best_right, moved_right, send_right = pick(score.astype(jnp.float32))
        busy_line = jnp.max(jnp.maximum(best_left, best_right), axis=0, keepdims=True)
        if step >= FIRST_OVER:
            here = ((left <= place) & (place < home)) | ((right >= place) & (place > home))
            best_over, moved_over, send_over = pick(jnp.where(here, wanted * (count - ids).astype(jnp.float32), 0.0))
            wanted = wanted - moved_over
            busy = jnp.maximum(busy_line, jnp.max(best_over, axis=0, keepdims=True))
        else:
            send_over, busy = jnp.full((line, 1), float(count), jnp.float32), busy_line
        for i, send in enumerate((send_left, send_right, send_over)):
            table_ref[3 * step + i] = send.astype(jnp.int32)
        if step <= opened:
            first = jnp.where(even, send_right, send_left)
            second = jnp.where(even, send_left, send_right)
            for i, send in enumerate((first, second, send_over)):
                name = write(3 * step + i, send)
                if i == 2 and step >= FIRST_OVER:
                    gone.append(name)
            come_left, come_right = of(send_left, me + 1), of(send_right, me - 1)
            names += [jnp.where(even, come_left, come_right), jnp.where(even, come_right, come_left)]
        left = left - anywhere(moved_left)
        right = right + anywhere(moved_right)
        length = jnp.where(jnp.where(lane == 0, busy_line, busy) > 0.0, step + 1, length)
    length_ref[0] = jnp.max(length[:, :1].astype(jnp.float32)).astype(jnp.int32)
    length_ref[1] = jnp.max(length[:, 1:].astype(jnp.float32)).astype(jnp.int32)

    names = names[: owned + 2 * opened]
    row = 0
    for side, queue in ((0, names), (1, names), (0, gone)):
        for n in range(owned):
            scales = [
                jnp.where(ours[side] == me * owned + n, (codes_ref[t].astype(jnp.float32) - 3.5) * 0.5, 0.0)
                for t, ours in enumerate(pairs)
            ]
            for name in queue:
                weight = jnp.zeros((1, 1), jnp.float32)
                for scale, ours in zip(scales, pairs):
                    weight = weight + jnp.where(name == ours[1 - side], scale, 0.0)
                weight_ref[row] = jnp.broadcast_to(weight, weight_ref.shape[1:])
                row += 1


def plan_rounds(me, term_nodes, weight_codes, line, owned, rounds, opened, cols):
    overs = opened + 1 - FIRST_OVER
    rows = owned * (2 * (owned + 2 * opened) + overs)
    slots, weights, tables, lengths = pl.pallas_call(
        functools.partial(plan_kernel, line, owned, term_nodes.shape[1], rounds, opened),
        out_shape=[
            jax.ShapeDtypeStruct((3 * (opened + 1), 1, 128), jnp.float32),
            jax.ShapeDtypeStruct((rows, 1, cols), jnp.float32),
            jax.ShapeDtypeStruct((3 * rounds, line, 1), jnp.int32),
            jax.ShapeDtypeStruct((2,), jnp.int32),
        ],
        in_specs=[pl.BlockSpec(memory_space=space) for space in (pltpu.SMEM, pl.ANY, pltpu.SMEM)],
        scratch_shapes=[pltpu.SMEM(term_nodes.shape, jnp.int32), pltpu.SemaphoreType.DMA],
        out_specs=[pl.BlockSpec(memory_space=pltpu.VMEM)] * 3 + [pl.BlockSpec(memory_space=pltpu.SMEM)],
        cost_estimate=pl.CostEstimate(flops=1000, bytes_accessed=1000, transcendentals=0),
    )(me, term_nodes, weight_codes)
    return slots, weights, tables, lengths


def split(value):
    high = value.astype(jnp.bfloat16)
    return high, (value - high.astype(jnp.float32)).astype(jnp.bfloat16)


def product(left, right_real, right_imag):
    rows = left.shape[2]
    every = left.reshape(4 * rows, left.shape[3])
    dot = functools.partial(jnp.dot, preferred_element_type=jnp.float32)

    def times(high, low):
        one, two = dot(every, high), dot(every[: 2 * rows], low)
        both = one[: 2 * rows] + (one[2 * rows :] + two)
        return both[:rows], both[rows:]

    real_real, imag_real = times(*right_real)
    real_imag, imag_imag = times(*right_imag)
    return real_real - imag_imag, real_imag + imag_real


def put_left(ref, n, c, cols, value):
    for part, piece in enumerate(split(value)):
        ref[n, part, c, :, cols] = piece


def put_right(ref, n, c, rows, value):
    for part, piece in enumerate(split(value)):
        ref[n, c, part, rows, :] = piece


def right_parts(ref, n):
    return [(ref[n, c, 0], ref[n, c, 1]) for c in range(2)]


def block(index, size):
    return pl.ds(pl.multiple_of(index * size, size), size)


def fetch(terms_ref, terms_here, sem):
    copy = pltpu.make_async_copy(terms_ref, terms_here, sem)
    copy.start()
    copy.wait()


def copy_chosen(slots, nodes, outs, sems):
    for i, (slot, out_ref) in enumerate(zip(slots, outs)):
        for k, node in enumerate(nodes):

            @pl.when(slot == k)
            def _(node=node, out_ref=out_ref, i=i):
                pltpu.make_async_copy(node, out_ref, sems.at[i]).start()

    return [pltpu.make_async_copy(nodes[0], out_ref, sems.at[i]) for i, out_ref in enumerate(outs)]


def first_kernel(line, owned, terms, place_ref, terms_ref, own_ref, first_ref, second_ref, *refs):
    copies, (terms_here, sem, sems) = refs[:owned], refs[owned:]
    moves = [
        pltpu.make_async_copy(own_ref.at[c, m], copies[m].at[c], sems.at[c, m]) for m in range(owned) for c in range(2)
    ]
    fetch = pltpu.make_async_copy(terms_ref, terms_here, sem)
    for move in [fetch, *moves]:
        move.start()
    fetch.wait()
    me = place_ref[0]
    choice = []
    zero = jnp.int32(0)
    lows, highs, low_seconds, high_seconds = [[zero] * owned for _ in range(4)]
    for t in range(terms):
        a, b = terms_here[0, t], terms_here[1, t]
        to_second, to_first = b // owned - me, a // owned - me
        for m in range(owned):
            name = me * owned + m
            away = jnp.where(a == name, to_second, jnp.where(b == name, to_first, 0))
            lows[m] = jnp.maximum(lows[m], -away)
            highs[m] = jnp.maximum(highs[m], away)
            low_seconds[m] = jnp.where((b == name) & (to_first < 0), 1, low_seconds[m])
            high_seconds[m] = jnp.where((b == name) & (to_first > 0), 1, high_seconds[m])
    for far, seconds in ((lows, low_seconds), (highs, high_seconds)):
        best, slot = jnp.int32(-1), zero
        for m in range(owned):
            score = jnp.where(far[m] > 0, 2 * far[m] + seconds[m], 0)
            slot = jnp.where(score > best, m, slot)
            best = jnp.maximum(score, best)
        choice.append(slot)
    even = lax.rem(me, 2) == 0
    slots = (jnp.where(even, choice[1], choice[0]), jnp.where(even, choice[0], choice[1]))
    for move in moves:
        move.wait()
    for slot, out_ref in zip(slots, (first_ref, second_ref)):
        for m in range(owned):

            @pl.when(slot == m)
            def _(m=m, out_ref=out_ref):
                out_ref[...] = copies[m][...]


def choose_kernel(rows, slot_ref, *refs):
    count = len(refs) - 1 - len(rows)
    slots = [jnp.max(slot_ref[row]).astype(jnp.int32) for row in rows]
    for copy in copy_chosen(slots, refs[:count], refs[count:-1], refs[-1]):
        copy.wait()


def early_kernel(subs, reps, names, place_ref, weight_ref, *refs):
    outs = 2 + subs - 1 + 2
    refs, (u_ref, v_ref, *rest) = refs[: len(refs) - outs], refs[len(refs) - outs :]
    x_refs, (row_ref, col_ref) = rest[: subs - 1], rest[subs - 1 :]
    own, beside, refs = refs[0], refs[1:reps], refs[reps:]
    rows, cols = own.shape[2:]
    owned = own.shape[1]
    across = [refs[m * (subs - 1) : (m + 1) * (subs - 1)] for m in range(owned)]
    arrived = refs[owned * (subs - 1) :]
    for n in range(owned):
        for c in range(2):
            for i in range(reps):
                at = block(place_ref[1 + subs + i], cols)
                put_left(row_ref, n, c, at, (own if i == 0 else beside[i - 1])[c, n])
            for i in range(subs):
                matrix = own[c, n] if i == 0 else across[n][i - 1][c]
                put_right(col_ref, n, c, block(place_ref[1 + i], rows), matrix)
            nodes = [own[c, m] for m in range(owned)] + [a[c] for a in arrived]
            u_ref[n, c] = sum(weight_ref[n * names + k] * node for k, node in enumerate(nodes))
            v_ref[n, c] = sum(weight_ref[(owned + n) * names + k] * node for k, node in enumerate(nodes))
            for j in range(subs - 1):
                x_refs[j][n, c] = sum(weight_ref[n * names + m] * across[m][j][c] for m in range(owned))


def sum_kernel(subs, reps, names, gone, seen, arrived, place_ref, weight_ref, row_ref, col_ref, *refs):
    u, v, refs = refs[:subs], refs[subs : subs + reps], refs[subs + reps :]
    came = [refs[i * arrived : (i + 1) * arrived] for i in range(reps)]
    items, over, (out_ref, left_ref, v_parts, u_parts) = came[0], refs[reps * arrived : -4], refs[-4:]
    rows, cols = out_ref.shape[2:]
    owned = out_ref.shape[0]
    for n in range(owned):
        for c in range(2):
            for i in range(subs):
                total = u[i][n, c]
                if i == 0:
                    for k, item in enumerate(items):
                        total = total + weight_ref[n * names + seen + k] * item[c]
                else:
                    for k, item in enumerate(over[i - 1 :: subs - 1]):
                        total = total + weight_ref[2 * owned * names + n * gone + k] * item[c]
                put_right(u_parts, n, c, block(place_ref[1 + i], rows), total)
            for i in range(reps):
                total = v[i][n, c]
                for k, item in enumerate(came[i]):
                    total = total + weight_ref[(owned + n) * names + seen + k] * item[c]
                put_left(v_parts, n, c, block(place_ref[1 + subs + i], cols), total)
        one = product(row_ref[n], *right_parts(u_parts, n))
        two = product(v_parts[n], *right_parts(col_ref, n))
        out_ref[n, 0] = one[0] + two[0]
        out_ref[n, 1] = one[1] + two[1]
        for j in range(subs - 1):
            left_ref[j, n] = row_ref[n, :, :, :, block(place_ref[2 + j], rows)]


def late_kernel(subs, first, stride, weight_ref, sum_ref, left_ref, *refs):
    over, out_ref = refs[: subs - 1], refs[subs - 1]
    for n in range(sum_ref.shape[0]):
        real, imag = sum_ref[n, 0], sum_ref[n, 1]
        for j in range(subs - 1):
            one = product(left_ref[j, n], *[split(weight_ref[first + stride * n] * over[j][c]) for c in range(2)])
            real, imag = real + one[0], imag + one[1]
        out_ref[n, 0] = real
        out_ref[n, 1] = imag


def times_resident(cells, i, place_ref, pick_ref, col_ref, s_ref, n):
    at = block(place_ref[1 + cells + i], s_ref.shape[3])
    node = pick_ref[place_ref[0] * s_ref.shape[0] + n]
    parts = [split(s_ref[n, c]) for c in range(2)]
    left = jnp.stack([jnp.stack([parts[c][part] for c in range(2)]) for part in range(2)])
    return product(left, *[(col_ref[node, c, 0, at, :], col_ref[node, c, 1, at, :]) for c in range(2)])


def half_kernel(cells, place_ref, pick_ref, col_ref, s_ref, out_ref):
    for n in range(s_ref.shape[0]):
        out_ref[0, n], out_ref[1, n] = times_resident(cells, 0, place_ref, pick_ref, col_ref, s_ref, n)


def last_kernel(cells, place_ref, pick_ref, col_ref, half_ref, *refs):
    for n in range(half_ref.shape[1]):
        real, imag = half_ref[0, n], half_ref[1, n]
        for i, s_ref in enumerate(refs[:-1]):
            one = times_resident(cells, 1 + i, place_ref, pick_ref, col_ref, s_ref, n)
            real, imag = real + one[0], imag + one[1]
        refs[-1][0, n] = real
        refs[-1][1, n] = imag


def way_kernel(groups, fixed, *refs):
    lengths, out_ref = refs[:groups], refs[groups]
    along, over = jnp.int32(0), jnp.int32(0)
    for length in lengths:
        along = jnp.maximum(along, length[0] - fixed)
        over = jnp.maximum(over, length[1] - fixed - 1)
    way = jnp.where(along > 0, 1, 0)
    way = jnp.where(over > 0, 2, way)
    out_ref[0] = jnp.where((along > 1) | (over > 1), 3, way)


def call(kernel, scalars, arrays, outs, scratch=()):
    return pl.pallas_call(
        kernel,
        out_shape=outs,
        in_specs=[pl.BlockSpec(memory_space=pltpu.SMEM)] * len(scalars)
        + [pl.BlockSpec(memory_space=pltpu.VMEM)] * len(arrays),
        out_specs=jax.tree.map(lambda _: pl.BlockSpec(memory_space=pltpu.VMEM), outs),
        scratch_shapes=list(scratch),
        compiler_params=pltpu.CompilerParams(vmem_limit_bytes=VMEM_BYTES),
        cost_estimate=pl.CostEstimate(flops=1000, bytes_accessed=1000, transcendentals=0),
    )(*scalars, *arrays)


def shifts(array, axis):
    size = lax.axis_size(axis)
    return [lax.ppermute(array, axis, [(i, (i + j) % size) for i in range(size)]) for j in range(1, size)]


def places(axis):
    size = lax.axis_size(axis)
    return [(lax.axis_index(axis) - j) % size for j in range(size)]


def body(meson_nodes, term_nodes, weight_codes, resident_pick):
    line = lax.axis_size("node")
    subs, reps = lax.axis_size("sub"), lax.axis_size("rep")
    _, owned, rows, cols = meson_nodes.shape
    count = owned * line
    terms = term_nodes.shape[0]
    me = lax.axis_index("node")
    base = me * owned
    to_left = [(z + 1, z) for z in range(line - 1)]
    to_right = [(z, z + 1) for z in range(line - 1)]
    node_shape = (2, rows, cols)
    nodes_shape = (owned, 2, rows, cols)
    depth = rows * subs
    fixed = min(line - 1, UNROLLED)
    opened = fixed + 1

    def out(shape, dtype=jnp.float32):
        return jax.ShapeDtypeStruct(shape, dtype)

    def near(shape, dtype=jnp.float32):
        return pltpu.VMEM(shape, dtype)

    place = jnp.stack([me, *places("sub"), *places("rep")]).astype(jnp.int32)
    slots, weights, tables, length = plan_rounds(
        place, term_nodes.T, weight_codes, line, owned, round_bound(line, owned, terms), opened, cols
    )

    names = owned + 2 * opened
    gone = opened + 1 - FIRST_OVER
    pairs = [[(z, z + 1) for z in range(start, line - 1, 2)] for start in range(2)]
    swaps = [pair + [(j, i) for i, j in pair] for pair in pairs]

    def choose(step, kinds, came):
        nodes = [*own, *came]
        return pl.pallas_call(
            functools.partial(choose_kernel, [3 * step + kind for kind in kinds]),
            out_shape=[out(node_shape)] * len(kinds),
            in_specs=[pl.BlockSpec(memory_space=pltpu.VMEM)] + [pl.BlockSpec(memory_space=pl.ANY)] * len(nodes),
            out_specs=[pl.BlockSpec(memory_space=pltpu.VMEM)] * len(kinds),
            scratch_shapes=[pltpu.SemaphoreType.DMA((len(kinds),))],
            compiler_params=pltpu.CompilerParams(vmem_limit_bytes=VMEM_BYTES),
            cost_estimate=pl.CostEstimate(flops=1000, bytes_accessed=1000, transcendentals=0),
        )(slots, *nodes)

    def meet(first, second):
        return [lax.ppermute(item, "node", swap) for item, swap in zip((first, second), swaps)]

    first, second, *own = pl.pallas_call(
        functools.partial(first_kernel, line, owned, terms),
        out_shape=[out(node_shape)] * (2 + owned),
        in_specs=[pl.BlockSpec(memory_space=space) for space in (pltpu.SMEM, pl.ANY, pl.ANY)],
        out_specs=[pl.BlockSpec(memory_space=pltpu.VMEM)] * (2 + owned),
        scratch_shapes=[
            pltpu.SMEM(term_nodes.shape[::-1], jnp.int32),
            pltpu.SemaphoreType.DMA,
            pltpu.SemaphoreType.DMA((2, owned)),
        ],
        compiler_params=pltpu.CompilerParams(vmem_limit_bytes=VMEM_BYTES),
        cost_estimate=pl.CostEstimate(flops=1000, bytes_accessed=1000, transcendentals=0),
    )(place, term_nodes.T, meson_nodes)
    came, across, over = [], [], []
    lengths = [length, *shifts(length, "grp")]
    for step in range(fixed):
        if step < FIRST_OVER:
            beyond = own[step : owned if step == FIRST_OVER - 1 else step + 1]
            if step > 0:
                first, second = choose(step, (0, 1), came)
        else:
            first, second, *beyond = choose(step, (0, 1, 2), came)
        beyond = [x for item in beyond for x in shifts(item, "sub")]
        new, beyond = lax.optimization_barrier((meet(first, second), beyond))
        came = came + new
        if step < FIRST_OVER:
            across = across + beyond
        else:
            over = over + beyond
        if step == FIRST_OVER - 1:
            beside = shifts(meson_nodes, "rep")
            came, beside, lengths = lax.optimization_barrier((came, beside, lengths))
            before = len(came)
            way = pl.pallas_call(
                functools.partial(way_kernel, len(lengths), fixed),
                out_shape=jax.ShapeDtypeStruct((1,), jnp.int32),
                in_specs=[pl.BlockSpec(memory_space=pltpu.SMEM)] * len(lengths),
                out_specs=pl.BlockSpec(memory_space=pltpu.SMEM),
            )(*lengths)

    row_part, col_part = (owned, 2, 2, rows, depth), (owned, 2, 2, depth, cols)

    def begin(beside, across, came):
        *mixed, row, col = call(
            functools.partial(early_kernel, subs, reps, names),
            [place],
            [weights, meson_nodes, *beside, *across, *came],
            [out(nodes_shape), near(nodes_shape)]
            + [out(nodes_shape)] * (subs - 1)
            + [out(row_part, jnp.bfloat16), out(col_part, jnp.bfloat16)],
        )
        return mixed, row, col

    early, row, col = begin(beside, across, came[:before])

    def sums(row, col, u, v, items=(), over=()):
        return call(
            functools.partial(sum_kernel, subs, reps, names, gone, owned + before, len(items) // reps),
            [place],
            [weights, row, col, *u, *v, *items, *over],
            [out(nodes_shape), out((subs - 1, owned, 2, 2, rows, rows), jnp.bfloat16)],
            [pltpu.VMEM(row_part, jnp.bfloat16), pltpu.VMEM(col_part, jnp.bfloat16)],
        )

    def beyond_rep(items):
        there = [shifts(item, "rep") for item in items]
        return [*items, *[each[j] for j in range(reps - 1) for each in there]]

    u, *ux = early[:1] + early[2:]

    def level(came, over):
        v = [early[1], *shifts(early[1], "rep")]
        return sums(row, col, [u, *ux], v, beyond_rep(came[before:]), over)

    def end(step, came, over):
        [item] = choose(step, (2,), came)
        late = shifts(item, "sub")
        first = 2 * owned * names + step - FIRST_OVER
        return call(
            functools.partial(late_kernel, subs, first, gone),
            [],
            [weights, *level(came, over), *late],
            out(nodes_shape),
        )

    def short(_):
        return end(fixed, came, over)

    def one_more():
        first, second, item = choose(fixed, (0, 1, 2), came)
        new, beyond = lax.optimization_barrier((meet(first, second), shifts(item, "sub")))
        return came + new, over + beyond

    def middle(_):
        return level(*one_more())[0]

    def middle_end(_):
        return end(fixed + 1, *one_more())

    def long(_):
        edges = jnp.pad(tables.reshape(-1, 3, line), ((0, 0), (0, 0), (1, 1)), constant_values=count)
        mine = lax.dynamic_slice_in_dim(edges, me, 3, axis=2)
        rounds = functools.reduce(jnp.maximum, [length[1] for length in lengths])
        leading, trailing = term_nodes[:, 0], term_nodes[:, 1]
        factors = (weight_codes.astype(jnp.float32) - 3.5) * 0.5
        mine_ids = base + jnp.arange(owned, dtype=jnp.int32)
        first_mine = factors[:, None] * (leading[:, None] == mine_ids)
        second_mine = factors[:, None] * (trailing[:, None] == mine_ids)
        held = jnp.zeros((count + 1, 2, rows, cols), jnp.float32)
        held = lax.dynamic_update_slice(held, jnp.swapaxes(meson_nodes, 0, 1), (base, 0, 0, 0))
        across = [x for m in range(owned) for x in shifts(meson_nodes[:, m], "sub")]
        (u, v, *ux), row, col = begin(shifts(meson_nodes, "rep"), across, [])

        def add(total, mine_terms, others, name, item):
            scale = jnp.sum(mine_terms * (others == name)[:, None], axis=0)
            return total + scale[:, None, None, None] * item[None]

        def more(state):
            return state[0] < rounds

        def again(state):
            step, held, u, v = state
            ids = lax.dynamic_index_in_dim(mine, step, 0, keepdims=False)
            left, right, item = lax.optimization_barrier(
                tuple(lax.dynamic_index_in_dim(held, ids[i, 1], 0, keepdims=False) for i in range(3))
            )
            from_right = lax.ppermute(left, "node", to_left)
            from_left = lax.ppermute(right, "node", to_right)
            items = [item, *shifts(item, "sub")]
            from_right, from_left = lax.optimization_barrier((from_right, from_left))
            u = [add(total, first_mine, trailing, ids[2, 1], x) for total, x in zip(u, items)]
            v = add(v, second_mine, leading, ids[0, 2], from_right)
            v = add(v, second_mine, leading, ids[1, 0], from_left)
            held = lax.dynamic_update_slice_in_dim(held, from_right[None], ids[0, 2], 0)
            held = lax.dynamic_update_slice_in_dim(held, from_left[None], ids[1, 0], 0)
            return step + 1, held, u, v

        _, _, u, v = lax.while_loop(more, again, (jnp.int32(0), held, [u, *ux], v))
        return sums(row, col, u, [v, *shifts(v, "rep")])[0]

    summed = lax.switch(way[0], [short, middle, middle_end, long], None)
    half = call(functools.partial(half_kernel, subs), [place, resident_pick], [col, summed], out(meson_nodes.shape))
    return call(
        functools.partial(last_kernel, subs),
        [place, resident_pick],
        [col, half, *shifts(summed, "rep")],
        out(meson_nodes.shape),
    )


def solution(mesh):
    in_specs = (P(None, ("grp", "node"), "sub", "rep"), P("grp", None), P("grp"), P("grp"))
    out_specs = P(None, ("grp", "node"), "sub", "rep")
    return jax.shard_map(body, mesh=mesh, in_specs=in_specs, out_specs=out_specs, check_vma=False)
```
